256 devices in a mesh: win: 8 (over y, core), pair: 32 (over x, z).
Axes of the slice: x: 4, y: 4, z: 8, core: 2. Of those that a mesh axis runs over, the one named last changes fastest.
Arguments:
- spectra: bfloat16 [8, 1024, 2, 8192], P('win', 'pair'), may hold values from -130 to 130
- availability: int32 [8, 1024], P('win', 'pair'), may hold values from 0 to 1
- owners: int32 [32, 32], replicated, may hold values from 0 to 1023, as said below
Outputs:
- correlations: float32 [16, 512, 512], P('win', 'pair')
The draws below stay inside these ranges and needn't reach their ends.
Inputs may be any that keep to these rules, and one draw needn't show every extreme that they name: `owners`: entries are station numbers below 1024; the 32 stations of a row are distinct; a row takes at most 2 stations from one block of 32 stations (stations s with equal s // 32), and exactly 2 from at least one block.
All inputs are finite; a program needn't handle non-finite values.
Results may differ from the reference program's by a relative error of at most 0.0085.
Values may be sent and summed in bfloat16 or wider, within the bound.
A program may use at most 64 MiB of HBM per device.

```python
import math
import jax
import jax.numpy as jnp
from jax import lax

F = 8192
WB = 64
LAGS = 512
PR = 16
PC = 16
WD = 1
SD = 32
NEED = 32
BLOCKS = 32
CAP = 2
WINDOWS = 8
STATIONS = 1024


def draw_spectra(key, part):
    key = jax.random.fold_in(key, 11)
    key_base, key_level = jax.random.split(key, 2)
    band_total = F // WB
    level = jnp.exp(jax.random.uniform(key_level, (WINDOWS, STATIONS, 1, band_total), jnp.float32, 0.0, math.log(10.0)))
    base = jnp.clip(jax.random.normal(key_base, (WINDOWS, STATIONS, 2, F), jnp.float32), -6.0, 6.0)
    level = jnp.repeat(level, WB, axis=3)
    return (base * level).astype(jnp.bfloat16)


def draw_availability(key, part):
    key = jax.random.fold_in(key, 12)
    key_kind, key_cut, key_drop = jax.random.split(key, 3)
    station_kind = jax.random.randint(key_kind, (STATIONS,), 0, 3)
    cut_window = jax.random.randint(key_cut, (STATIONS,), 1, WINDOWS)
    window_index = lax.iota(jnp.int32, WINDOWS)[:, None]
    early = window_index < cut_window[None, :]
    span = jnp.where(station_kind[None, :] == 0, True, jnp.where(station_kind[None, :] == 1, early, jnp.logical_not(early)))
    kept = jax.random.randint(key_drop, (WINDOWS, STATIONS), 0, 8) != 0
    return jnp.logical_and(span, kept).astype(jnp.int32)


def draw_owners(key, part):
    key = jax.random.fold_in(key, 13)
    slot_total = BLOCKS * CAP

    def one_owner(owner_key):
        key_full, key_score, key_perm, key_order = jax.random.split(owner_key, 4)
        full_block = jax.random.randint(key_full, (), 0, BLOCKS)
        slot_ids = lax.iota(jnp.int32, slot_total)
        score = jax.random.randint(key_score, (slot_total,), 0, 1 << 20) * slot_total + slot_ids
        score = jnp.where(slot_ids // CAP == full_block, slot_ids % CAP - CAP, score)
        chosen = jnp.argsort(score, stable=True)[:NEED]
        block_of = chosen // CAP
        within = chosen % CAP
        perm_score = jax.random.randint(key_perm, (BLOCKS, SD), 0, 1 << 20) * SD + lax.iota(jnp.int32, SD)[None, :]
        perm = jnp.argsort(perm_score, axis=1, stable=True).astype(jnp.int32)
        station_ids = block_of * SD + perm[block_of, within]
        order_score = jax.random.randint(key_order, (NEED,), 0, 1 << 20) * NEED + lax.iota(jnp.int32, NEED)
        order = jnp.argsort(order_score, stable=True)
        return station_ids[order].astype(jnp.int32)
    return jax.vmap(one_owner)(jax.random.split(key, BLOCKS))


def setup_inputs(seed: int = 0) -> dict:
    splits = jax.random.split(jax.random.key(seed), 4)
    return {
        "spectra": draw_spectra(jax.random.fold_in(splits[3], 71), 0),
        "availability": draw_availability(jax.random.fold_in(splits[3], 71), 0),
        "owners": draw_owners(jax.random.fold_in(splits[3], 71), 0),
    }


EPSILON = 1e-06

def whiten(spectra, availability):
    values = spectra.astype(jnp.float32)
    magnitude = jnp.sqrt(values[..., 0, :] * values[..., 0, :] + values[..., 1, :] * values[..., 1, :])
    bin_total = magnitude.shape[-1]
    banded = magnitude.reshape(magnitude.shape[:-1] + (bin_total // WB, WB))
    band_level = lax.optimization_barrier(jnp.mean(banded, axis=-1)) + EPSILON
    factor = availability.astype(jnp.float32)[..., None] / band_level
    factor = jnp.repeat(factor, WB, axis=-1)
    return (values * factor[..., None, :]).astype(jnp.bfloat16)

def lag_table(first_bin, bin_width, bin_count, lag_count):
    period = 2 * bin_count
    bin_index = first_bin + lax.iota(jnp.int32, bin_width)
    lag_offset = (lax.iota(jnp.int32, lag_count) - lag_count // 2) % period
    phase_index = bin_index[:, None] * lag_offset[None, :] % period
    angles = phase_index.astype(jnp.float32) * (2.0 * math.pi / period)
    weight = jnp.where(bin_index == 0, 1.0, 2.0).astype(jnp.float32)[:, None] / math.sqrt(period)
    return jnp.concatenate([weight * jnp.cos(angles), -weight * jnp.sin(angles)], axis=0).astype(jnp.bfloat16)

def reference(spectra, availability, owners):
    groups = WINDOWS // WD
    bin_count = spectra.shape[3]
    full_table = lag_table(0, bin_count, bin_count, LAGS).astype(jnp.float32)

    def per_owner(own_row):
        chosen = jnp.take(spectra, own_row, axis=1)
        chosen_masks = jnp.take(availability, own_row, axis=1)
        whitened = whiten(chosen, chosen_masks).astype(jnp.float32)
        grouped = whitened.reshape(groups, WD, NEED, 2, bin_count)
        row_re = grouped[:, :, :PR, 0]
        row_im = grouped[:, :, :PR, 1]
        col_re = grouped[:, :, PR:, 0]
        col_im = grouped[:, :, PR:, 1]
        real_part = jnp.einsum('gwrf,gwcf->gcrf', row_re, col_re) + jnp.einsum('gwrf,gwcf->gcrf', row_im, col_im)
        imag_part = jnp.einsum('gwrf,gwcf->gcrf', row_im, col_re) - jnp.einsum('gwrf,gwcf->gcrf', row_re, col_im)
        partial_value = jnp.stack([real_part, imag_part], axis=3).astype(jnp.bfloat16)
        partial_value = lax.optimization_barrier(partial_value)
        stacked = lax.optimization_barrier(jnp.sum(partial_value.astype(jnp.float32), axis=0))
        lagged = jnp.dot(stacked.reshape(PC * PR, 2 * bin_count), full_table, precision=lax.Precision.HIGHEST, preferred_element_type=jnp.float32).reshape(PC, PR, LAGS)
        mask_values = chosen_masks.astype(jnp.float32)
        tallies = jnp.einsum('wc,wr->cr', mask_values[:, PR:], mask_values[:, :PR])
        return lagged / jnp.maximum(tallies, 1.0)[:, :, None]
    result = lax.map(per_owner, owners)
    return jnp.transpose(result, (1, 0, 2, 3)).reshape(PC, BLOCKS * PR, LAGS)
```

```python
import functools
import math

import jax
import jax.numpy as jnp
from jax import lax
from jax.experimental import pallas as pl
from jax.experimental.pallas import tpu as pltpu
from jax.sharding import PartitionSpec as P

WB = 64
LAGS = 512
PR = 16
PC = 16
NEED = 32
EPSILON = 1e-06

NX, NZ = 4, 8
N_PAIR = NX * NZ
N_WIN = 8
BLOCK = 32
BINS = 8192
CHUNK = BINS // N_WIN
SUBS = 4
SUB = CHUNK // SUBS
MSG = 16
ROWS = N_PAIR * MSG
PERIOD = 2 * BINS
FINE = 32

f32 = jnp.float32
bf16 = jnp.bfloat16
i32 = jnp.int32

OFFSETS = [
    (dx, dz) for dz in (4, 3, -3, 2, -2, 1, -1, 0) for dx in (2, 1, -1, 0) if (dx, dz) != (0, 0)
]


def iota(shape, dim):
    return lax.broadcasted_iota(i32, shape, dim)


def kernel(
    x_ref,
    own_ref,
    avail_ref,
    out_ref,
    recv1,
    send2,
    recv2,
    table,
    lhs,
    acc,
    smat,
    rmat,
    cos_a,
    sin_a,
    mask_send,
    mask_recv,
    tal_send,
    tal_recv,
    lag_send,
    lag_recv,
    s1_send,
    s1_recv,
    s2_send,
    s2_recv,
    m_send,
    m_recv,
    t_send,
    t_recv,
    l_send,
    l_recv,
):
    me_w = lax.axis_index("win")
    me_p = lax.axis_index("pair")
    x, z = me_p // NZ, me_p % NZ
    pair_peers = [((x + dx + NX) % NX) * NZ + (z + dz + NZ) % NZ for dx, dz in OFFSETS]

    def win_peer(t):
        return (me_w + t) % N_WIN

    barrier = pltpu.get_barrier_semaphore()
    for q in pair_peers:
        pl.semaphore_signal(barrier, inc=1, device_id={"pair": q})
    for t in range(1, N_WIN):
        pl.semaphore_signal(barrier, inc=1, device_id={"win": win_peer(t)})

    owners = own_ref[...]
    spread = (iota((ROWS, N_PAIR), 0) // MSG == iota((ROWS, N_PAIR), 1)).astype(bf16)
    block = jnp.dot(spread, (owners // BLOCK).astype(bf16), preferred_element_type=f32).astype(i32)
    station = jnp.dot(spread, (owners % BLOCK).astype(bf16), preferred_element_type=f32).astype(i32)
    mine = block == me_p
    first = jnp.min(jnp.where(mine, station, BLOCK - 1), axis=1, keepdims=True)
    last = jnp.max(jnp.where(mine, station, 0), axis=1, keepdims=True)
    row = iota((ROWS, 1), 0) % MSG
    wanted = jnp.where((row % 4) // 2 == 0, first, last)
    source = (row // 4) * (2 * BLOCK) + 2 * wanted + row % 2
    smat[...] = (iota((ROWS, SUBS * 2 * BLOCK), 1) == source).astype(bf16)
    mask_row = avail_ref[...].astype(f32)
    mask_send[...] = jnp.concatenate([mask_row, jnp.zeros((1, 128 - BLOCK), f32)], axis=1)
    mask_recv[me_p] = mask_send[...]

    pl.semaphore_wait(barrier, len(pair_peers) + N_WIN - 1)

    def phase1(t):
        chunk = pl.ds(pl.multiple_of(win_peer(t) * CHUNK, CHUNK), CHUNK)
        return pltpu.make_async_remote_copy(
            src_ref=x_ref.at[:, chunk],
            dst_ref=recv1.at[t],
            send_sem=s1_send.at[t],
            recv_sem=s1_recv.at[t],
            device_id={"win": win_peer(t)},
        )

    for t in range(1, N_WIN):
        phase1(t).start()

    def send_window(t, block_value):
        stacked = jnp.concatenate(
            [block_value[:, SUB * s : SUB * (s + 1)] for s in range(SUBS)], axis=0
        )
        message = jnp.dot(smat[...], stacked, preferred_element_type=f32).astype(bf16)
        send2[t] = message
        here = pl.ds(pl.multiple_of(me_p * MSG, MSG), MSG)
        for q in pair_peers:
            there = pl.ds(pl.multiple_of(q * MSG, MSG), MSG)
            pltpu.make_async_remote_copy(
                src_ref=send2.at[t, there],
                dst_ref=recv2.at[t, here],
                send_sem=s2_send.at[t],
                recv_sem=s2_recv.at[t],
                device_id={"pair": q},
            ).start()
        recv2[t, here, :] = send2[t, here, :]

    own_chunk = pl.ds(pl.multiple_of(me_w * CHUNK, CHUNK), CHUNK)
    send_window(0, x_ref[:, own_chunk])
    for q in pair_peers:
        pltpu.make_async_remote_copy(
            src_ref=mask_send,
            dst_ref=mask_recv.at[me_p],
            send_sem=m_send,
            recv_sem=m_recv,
            device_id={"pair": q},
        ).start()

    own_row = own_ref[pl.ds(me_p, 1), :]

    def pick(rows, lane):
        hit = iota((rows, NEED), 1) == lane
        return jnp.sum(jnp.where(hit, own_row, 0), axis=1, keepdims=True)

    sel_rows = SUBS * 2 * NEED
    sel = iota((sel_rows, 1), 0)
    chosen = pick(sel_rows, sel % NEED)
    earlier = jnp.logical_and(own_row // BLOCK == chosen // BLOCK, own_row < chosen)
    slot = jnp.max(earlier.astype(i32), axis=1, keepdims=True)
    target = (
        (chosen // BLOCK) * MSG + (sel // (2 * NEED)) * 4 + slot * 2 + (sel // NEED) % 2
    )
    rmat[...] = (iota((sel_rows, ROWS), 1) == target).astype(bf16)
    band = jnp.where(
        iota((SUB, SUB), 0) // WB == iota((SUB, SUB), 1) // WB, 1.0 / WB, 0.0
    ).astype(bf16)

    lag = iota((FINE, LAGS), 1) - LAGS // 2
    index = iota((FINE, LAGS), 0)

    def angle(phase):
        phase = jnp.bitwise_and(phase + PERIOD // 2, PERIOD - 1) - PERIOD // 2
        return phase.astype(f32) * (2.0 * math.pi / PERIOD)

    coarse = angle((me_w * CHUNK + FINE * index) * lag)
    cos_a[...] = jnp.cos(coarse)
    sin_a[...] = jnp.sin(coarse)
    fine = angle(index * lag)
    cos_b, sin_b = jnp.cos(fine), jnp.sin(fine)

    def table_rows(n, carry):
        ca, sa = cos_a[pl.ds(n, 1), :], sin_a[pl.ds(n, 1), :]
        bins = me_w * CHUNK + FINE * n + iota((FINE, 1), 0)
        weight = jnp.where(bins == 0, 1.0, 2.0) / math.sqrt(PERIOD)
        at = pl.multiple_of(n * FINE, FINE)
        table[pl.ds(at, FINE), :] = (weight * (ca * cos_b - sa * sin_b)).astype(bf16)
        table[pl.ds(CHUNK + at, FINE), :] = (-weight * (sa * cos_b + ca * sin_b)).astype(bf16)
        return carry

    lax.fori_loop(0, CHUNK // FINE, table_rows, 0)

    def relay(t, carry):
        phase1(t).wait_recv()
        send_window(t, recv1[t])
        return carry

    lax.fori_loop(1, N_WIN, relay, 0)

    pltpu.make_async_copy(
        mask_recv.at[pl.ds(0, N_PAIR - 1)], mask_recv.at[pl.ds(0, N_PAIR - 1)], m_recv
    ).wait()
    masks = mask_recv[:, 0, :].astype(bf16)
    pairs = PC * PR
    pair = iota((pairs, 1), 0)

    def mask_of(lane):
        who = pick(pairs, lane)
        where = (iota((pairs, N_PAIR), 1) == who // BLOCK).astype(bf16)
        lines = jnp.dot(where, masks, preferred_element_type=f32)
        hit = iota((pairs, 128), 1) == who % BLOCK
        return jnp.sum(jnp.where(hit, lines, 0.0), axis=1, keepdims=True)

    both = mask_of(pair % PR) * mask_of(PR + pair // PR)
    tal_send[...] = jnp.broadcast_to(both, (pairs, 128)).astype(bf16)
    share = pairs // N_WIN

    def tally(t):
        rows = pl.ds(pl.multiple_of(win_peer(t) * share, share), share)
        return pltpu.make_async_remote_copy(
            src_ref=tal_send.at[rows],
            dst_ref=tal_recv.at[t],
            send_sem=t_send.at[t],
            recv_sem=t_recv.at[t],
            device_id={"win": win_peer(t)},
        )

    for t in range(1, N_WIN):
        tally(t).start()

    acc[...] = jnp.zeros_like(acc)

    def window(t, carry):
        others = recv2.at[t, pl.ds(0, ROWS - MSG)]
        pltpu.make_async_copy(others, others, s2_recv.at[t]).wait()
        chosen_rows = jnp.dot(rmat[...], recv2[t], preferred_element_type=f32)
        for s in range(SUBS):
            re = chosen_rows[2 * NEED * s : 2 * NEED * s + NEED]
            im = chosen_rows[2 * NEED * s + NEED : 2 * NEED * (s + 1)]
            magnitude = jnp.sqrt(re * re + im * im)
            upper = magnitude.astype(bf16)
            lower = (magnitude - upper.astype(f32)).astype(bf16)
            level = jnp.dot(upper, band, preferred_element_type=f32) + jnp.dot(
                lower, band, preferred_element_type=f32
            )
            factor = 1.0 / (level + EPSILON)
            white_re = (re * factor).astype(bf16).astype(f32)
            white_im = (im * factor).astype(bf16).astype(f32)
            ar, ai = white_re[:PR], white_im[:PR]
            for j in range(PC):
                br, bi = white_re[PR + j : PR + j + 1], white_im[PR + j : PR + j + 1]
                rows = slice(PR * j, PR * (j + 1))
                lhs[rows, SUB * s : SUB * (s + 1)] = (ar * br + ai * bi).astype(bf16)
                lhs[rows, CHUNK + SUB * s : CHUNK + SUB * (s + 1)] = (ai * br - ar * bi).astype(
                    bf16
                )
        acc[...] += jnp.dot(lhs[...], table[...], preferred_element_type=f32)
        return carry

    lax.fori_loop(0, N_WIN, window, 0)

    lag_send[...] = acc[...].astype(bf16)

    def lagged(t):
        rows = pl.ds(pl.multiple_of(win_peer(t) * share, share), share)
        return pltpu.make_async_remote_copy(
            src_ref=lag_send.at[rows],
            dst_ref=lag_recv.at[t],
            send_sem=l_send.at[t],
            recv_sem=l_recv.at[t],
            device_id={"win": win_peer(t)},
        )

    for t in range(1, N_WIN):
        lagged(t).start()
    own = pl.ds(pl.multiple_of(me_w * share, share), share)
    count = tal_send[own, :].astype(f32)
    for t in range(1, N_WIN):
        tally(t).wait_recv()
        count = count + tal_recv[t].astype(f32)
    total = acc[own, :]
    for t in range(1, N_WIN):
        lagged(t).wait_recv()
        total = total + lag_recv[t].astype(f32)
    out_ref[...] = total / jnp.maximum(count[:, :1], 1.0)

    for t in range(1, N_WIN):
        phase1(t).wait_send()
        tally(t).wait_send()
        lagged(t).wait_send()
    pltpu.make_async_copy(
        mask_recv.at[pl.ds(0, N_PAIR - 1)], mask_recv.at[pl.ds(0, N_PAIR - 1)], m_send
    ).wait()
    for t in range(N_WIN):
        others = send2.at[t, pl.ds(0, ROWS - MSG)]
        pltpu.make_async_copy(others, others, s2_send.at[t]).wait()


def per_device(spectra, availability, owners):
    masked = spectra[0] * availability[0].astype(bf16)[:, None, None]
    masked = masked.reshape(2 * BLOCK, BINS)
    pairs = PC * PR
    share = pairs // N_WIN
    dma = pltpu.SemaphoreType.DMA
    vmem = pl.BlockSpec(memory_space=pltpu.VMEM)
    out = pl.pallas_call(
        kernel,
        out_shape=jax.ShapeDtypeStruct((share, LAGS), f32),
        in_specs=[vmem] * 3,
        out_specs=vmem,
        scratch_shapes=[
            pltpu.VMEM((N_WIN, 2 * BLOCK, CHUNK), bf16),
            pltpu.VMEM((N_WIN, ROWS, SUB), bf16),
            pltpu.VMEM((N_WIN, ROWS, SUB), bf16),
            pltpu.VMEM((2 * CHUNK, LAGS), bf16),
            pltpu.VMEM((pairs, 2 * CHUNK), bf16),
            pltpu.VMEM((pairs, LAGS), f32),
            pltpu.VMEM((ROWS, SUBS * 2 * BLOCK), bf16),
            pltpu.VMEM((SUBS * 2 * NEED, ROWS), bf16),
            pltpu.VMEM((CHUNK // FINE, LAGS), f32),
            pltpu.VMEM((CHUNK // FINE, LAGS), f32),
            pltpu.VMEM((1, 128), f32),
            pltpu.VMEM((N_PAIR, 1, 128), f32),
            pltpu.VMEM((pairs, 128), bf16),
            pltpu.VMEM((N_WIN, share, 128), bf16),
            pltpu.VMEM((pairs, LAGS), bf16),
            pltpu.VMEM((N_WIN, share, LAGS), bf16),
            dma((N_WIN,)),
            dma((N_WIN,)),
            dma((N_WIN,)),
            dma((N_WIN,)),
            dma,
            dma,
            dma((N_WIN,)),
            dma((N_WIN,)),
            dma((N_WIN,)),
            dma((N_WIN,)),
        ],
        compiler_params=pltpu.CompilerParams(
            collective_id=0, has_side_effects=True, vmem_limit_bytes=48 * 1024 * 1024
        ),
        cost_estimate=pl.CostEstimate(
            flops=6_000_000_000, bytes_accessed=2_000_000, transcendentals=1_000_000
        ),
    )(masked, owners, availability)
    return out.reshape(PC // N_WIN, PR, LAGS)


def solution(mesh):
    return jax.shard_map(
        per_device,
        mesh=mesh,
        in_specs=(P("win", "pair", None, None), P("win", "pair"), P()),
        out_specs=P("win", "pair", None),
        check_vma=False,
    )
```

```python
import math

import jax
import jax.numpy as jnp
from jax import lax
from jax.experimental import pallas as pl
from jax.experimental.pallas import tpu as pltpu
from jax.sharding import PartitionSpec as P

WB = 64
LAGS = 512
PR = 16
PC = 16
NEED = 32
EPSILON = 1e-06

NX, NZ = 4, 8
N_PAIR = NX * NZ
N_WIN = 8
BLOCK = 32
BINS = 8192
CHUNK = BINS // NZ
STEPS = 4
SUB = CHUNK // STEPS
AHEAD = 2
PLANE = NX * N_WIN
HALVES = 2
QUAD = NZ // HALVES
MSG = 4 * NZ
PERIOD = 2 * BINS
FINE = 32
PAIRS = PC * PR
SHARE = PAIRS // N_WIN

f32 = jnp.float32
bf16 = jnp.bfloat16
i32 = jnp.int32

Z_OFFSETS = [4, 3, -3, 2, -2, 1, -1]
PLANE_OFFSETS = [(dw, dx) for dw in (4, 3, 5, 2, 6, 1, 7, 0) for dx in (2, 1, -1, 0)][:-1]


def iota(shape, dim):
    return lax.broadcasted_iota(i32, shape, dim)


def kernel(
    x_hbm,
    own_hbm,
    avail_hbm,
    out_ref,
    x_ref,
    own_ref,
    avail_ref,
    recv1,
    send2,
    recv2,
    table,
    white,
    lhs,
    acc,
    smat,
    cos_a,
    sin_a,
    mask_z,
    mask_all,
    present,
    final_present,
    lag_send,
    lag_held,
    lag_recv,
    in_sem,
    d_send,
    d_recv,
    s_send,
    s_recv,
    m_send,
    m_recv,
    l_send,
    l_recv,
    f_send,
    f_recv,
):
    me_w = lax.axis_index("win")
    me_p = lax.axis_index("pair")
    x, z = me_p // NZ, me_p % NZ
    z_peers = [(z + dz + NZ) % NZ for dz in Z_OFFSETS]
    plane_peers = [((me_w + dw) % N_WIN, (x + dx + NX) % NX) for dw, dx in PLANE_OFFSETS]

    barrier = pltpu.get_barrier_semaphore()
    for k in z_peers:
        pl.semaphore_signal(barrier, inc=1, device_id={"pair": x * NZ + k})
    for o, k in plane_peers:
        pl.semaphore_signal(barrier, inc=1, device_id={"win": o, "pair": k * NZ + z})
    own_in = pltpu.make_async_copy(own_hbm, own_ref, in_sem.at[0])
    avail_in = pltpu.make_async_copy(avail_hbm, avail_ref, in_sem.at[1])
    x_in = pltpu.make_async_copy(x_hbm.at[0], x_ref, in_sem.at[2])
    own_in.start()
    avail_in.start()
    x_in.start()
    avail_in.wait()
    mask_z[z] = jnp.concatenate(
        [avail_ref[...].astype(f32), jnp.zeros((1, 128 - BLOCK), f32)], axis=1
    )
    x_in.wait()
    pl.semaphore_wait(barrier, NZ - 1 + PLANE - 1)


    def spectra_step(s, k):
        bins = pl.ds(pl.multiple_of(k * CHUNK + s * SUB, SUB), SUB)
        return x_ref.at[:, :, bins]

    def start_spectra(s):
        for k in z_peers:
            pltpu.make_async_remote_copy(
                src_ref=spectra_step(s, k),
                dst_ref=recv1.at[s, z],
                send_sem=d_send.at[s],
                recv_sem=d_recv.at[s],
                device_id={"pair": x * NZ + k},
            ).start()
        pltpu.make_async_copy(spectra_step(s, z), recv1.at[s, z], d_recv.at[s]).start()

    for k in z_peers:
        pltpu.make_async_remote_copy(
            src_ref=mask_z.at[z],
            dst_ref=mask_z.at[z],
            send_sem=m_send.at[0],
            recv_sem=m_recv.at[0],
            device_id={"pair": x * NZ + k},
        ).start()

    for s in range(AHEAD):
        start_spectra(s)
    own_in.wait()

    rows = 16 * N_PAIR
    owners = own_ref[...]
    spread = (iota((rows, N_PAIR), 0) >> 4 == iota((rows, N_PAIR), 1)).astype(bf16)
    block = jnp.dot(spread, (owners >> 5).astype(bf16), preferred_element_type=f32)
    station = jnp.dot(spread, (owners & 31).astype(bf16), preferred_element_type=f32)
    row = iota((rows, 1), 0)
    near = (row >> 2) & 3
    upper_slot = ((row >> 1) & 1) == 1
    for half in range(HALVES):
        mine = block == (x * NZ + half * QUAD + near).astype(f32)
        first = jnp.min(jnp.where(mine, station, BLOCK - 1.0), axis=1, keepdims=True)
        last = jnp.max(jnp.where(mine, station, 0.0), axis=1, keepdims=True)
        wanted = jnp.where(upper_slot, last, first).astype(i32)
        source = near * (2 * BLOCK) + 2 * wanted + (row & 1)
        smat[half] = (iota((rows, QUAD * 2 * BLOCK), 1) == source).astype(bf16)

    near_masks = mask_z.at[pl.ds(0, NZ - 1)]
    pltpu.make_async_copy(near_masks, near_masks, m_recv.at[0]).wait()
    here = pl.ds((me_w * NX + x) * NZ, NZ)
    for o, k in plane_peers:
        pltpu.make_async_remote_copy(
            src_ref=mask_z,
            dst_ref=mask_all.at[here],
            send_sem=m_send.at[1],
            recv_sem=m_recv.at[1],
            device_id={"win": o, "pair": k * NZ + z},
        ).start()
    mask_all[here] = mask_z[...]
    far_masks = mask_all.at[pl.ds(0, N_WIN * N_PAIR - NZ)]

    def relay(s):
        whole = recv1.at[s]
        pltpu.make_async_copy(whole, whole, d_recv.at[s]).wait()

        @pl.when(s + AHEAD < STEPS)
        def _():
            start_spectra(s + AHEAD)

        for half in range(HALVES):
            stations = recv1[s, half * QUAD : (half + 1) * QUAD].reshape(QUAD * 2 * BLOCK, SUB)
            message = jnp.dot(smat[half], stations, preferred_element_type=f32).astype(bf16)
            send2[s, :, 16 * half : 16 * (half + 1), :] = message.reshape(N_PAIR, 16, SUB)
        for o, k in plane_peers:
            pltpu.make_async_remote_copy(
                src_ref=send2.at[s, k * NZ + o],
                dst_ref=recv2.at[s, me_w * NX + x],
                send_sem=s_send.at[s],
                recv_sem=s_recv.at[s],
                device_id={"win": o, "pair": k * NZ + z},
            ).start()
        recv2[s, me_w * NX + x] = send2[s, x * NZ + me_w]

    def process(s):
        others = recv2.at[s, pl.ds(0, PLANE - 1)]
        pltpu.make_async_copy(others, others, s_recv.at[s]).wait()
        for w in range(N_WIN):
            messages = recv2[s, NX * w : NX * (w + 1)].reshape(NX * MSG, SUB)
            lines = jnp.dot(rmat, messages, preferred_element_type=f32)
            re, im = lines[:NEED], lines[NEED:]
            magnitude = jnp.sqrt(re * re + im * im)
            upper = magnitude.astype(bf16)
            lower = (magnitude - upper.astype(f32)).astype(bf16)
            level = jnp.dot(upper, band, preferred_element_type=f32) + jnp.dot(
                lower, band, preferred_element_type=f32
            )
            factor = present[NEED * w : NEED * (w + 1), :1] / (level + EPSILON)
            white[w, 0] = (re * factor).astype(bf16).astype(f32)
            white[w, 1] = (im * factor).astype(bf16).astype(f32)
        for j in range(PC):
            total_re = jnp.zeros((PR, SUB), f32)
            total_im = jnp.zeros((PR, SUB), f32)
            for w in range(N_WIN):
                ar, ai = white[w, 0, :PR, :], white[w, 1, :PR, :]
                br = white[w, 0, PR + j : PR + j + 1, :]
                bi = white[w, 1, PR + j : PR + j + 1, :]
                total_re = total_re + (ar * br + ai * bi)
                total_im = total_im + (ai * br - ar * bi)
            for part, total in enumerate((total_re, total_im)):
                upper = total.astype(bf16)
                lower = (total - upper.astype(f32)).astype(bf16)
                lhs[PR * j : PR * (j + 1), SUB * part : SUB * (part + 1)] = upper
                lhs[PAIRS + PR * j : PAIRS + PR * (j + 1), SUB * part : SUB * (part + 1)] = lower
        product = jnp.dot(lhs[...], table[s], preferred_element_type=f32)
        acc[...] += product[:PAIRS] + product[PAIRS:]

    relay(0)

    lag = iota((FINE, LAGS), 1) - LAGS // 2
    index = iota((FINE, LAGS), 0)

    def angle(phase):
        phase = ((phase + PERIOD // 2) & (PERIOD - 1)) - PERIOD // 2
        return phase.astype(f32) * (2.0 * math.pi / PERIOD)

    coarse = angle((z * CHUNK + FINE * index) * lag)
    cos_a[...] = jnp.cos(coarse)
    sin_a[...] = jnp.sin(coarse)
    fine = angle(index * lag)
    cos_b, sin_b = jnp.cos(fine), jnp.sin(fine)

    def table_rows(n, carry):
        ca, sa = cos_a[pl.ds(n, 1), :], sin_a[pl.ds(n, 1), :]
        bins = z * CHUNK + FINE * n + iota((FINE, 1), 0)
        weight = jnp.where(bins == 0, 1.0, 2.0) / math.sqrt(PERIOD)
        s = n // (SUB // FINE)
        at = pl.multiple_of(n % (SUB // FINE) * FINE, FINE)
        table[s, pl.ds(at, FINE), :] = (weight * (ca * cos_b - sa * sin_b)).astype(bf16)
        table[s, pl.ds(SUB + at, FINE), :] = (-weight * (sa * cos_b + ca * sin_b)).astype(bf16)
        return carry

    lax.fori_loop(0, CHUNK // FINE, table_rows, 0)

    def pick(count, lane, own_row):
        hit = iota((count, NEED), 1) == lane
        return jnp.sum(jnp.where(hit, own_row, 0), axis=1, keepdims=True)

    work_row = own_ref[pl.ds(x * NZ + me_w, 1), :]
    sel = iota((2 * NEED, 1), 0)
    chosen = pick(2 * NEED, sel & (NEED - 1), work_row)
    earlier = jnp.logical_and(work_row >> 5 == chosen >> 5, work_row < chosen)
    slot = jnp.max(earlier.astype(f32), axis=1, keepdims=True).astype(i32)
    target = (chosen >> 5) * 4 + slot * 2 + (sel >> 5)
    rmat = (iota((2 * NEED, NX * MSG), 1) == target).astype(bf16)
    band = jnp.where(iota((SUB, SUB), 0) >> 6 == iota((SUB, SUB), 1) >> 6, 1.0 / WB, 0.0)
    band = band.astype(bf16)
    acc[...] = jnp.zeros_like(acc)

    line = iota((N_WIN * NEED, 1), 0)

    def availability_of(masks, own_row):
        who = pick(N_WIN * NEED, line & (NEED - 1), own_row)
        place = (line >> 5) * N_PAIR + (who >> 5)
        where = (iota((N_WIN * NEED, N_WIN * N_PAIR), 1) == place).astype(bf16)
        found = jnp.dot(where, masks, preferred_element_type=f32)
        hit = iota((N_WIN * NEED, 128), 1) == who & 31
        value = jnp.sum(jnp.where(hit, found, 0.0), axis=1, keepdims=True)
        return jnp.broadcast_to(value, (N_WIN * NEED, 128))


    def step(s, carry):
        @pl.when(s < STEPS)
        def _():
            relay(s)

        @pl.when(s == 1)
        def _():
            pltpu.make_async_copy(far_masks, far_masks, m_recv.at[1]).wait()
            masks = mask_all[:, 0, :].astype(bf16)
            present[...] = availability_of(masks, work_row)
            final_present[...] = availability_of(masks, own_ref[pl.ds(me_p, 1), :])

        process(s - 1)
        return carry

    lax.fori_loop(1, STEPS + 1, step, 0)

    lag_send[...] = acc[...].astype(bf16).reshape(N_WIN, SHARE, LAGS)

    def across(t):
        o = (me_w + t) % N_WIN
        return pltpu.make_async_remote_copy(
            src_ref=lag_send.at[o],
            dst_ref=lag_held.at[t],
            send_sem=l_send.at[t],
            recv_sem=l_recv.at[t],
            device_id={"win": o},
        )

    def along_remote(t, piece):
        owner = (me_w - t + N_WIN) % N_WIN
        return pltpu.make_async_remote_copy(
            src_ref=piece,
            dst_ref=lag_recv.at[z],
            send_sem=f_send.at[t],
            recv_sem=f_recv.at[z],
            device_id={"pair": x * NZ + owner},
        )

    def along(t, piece):
        owner = (me_w - t + N_WIN) % N_WIN

        @pl.when(owner == z)
        def _():
            pltpu.make_async_copy(piece, lag_recv.at[z], f_recv.at[z]).start()

        @pl.when(owner != z)
        def _():
            along_remote(t, piece).start()

    HOPS = (4, 3, 5, 2, 6, 1, 7)
    for t in HOPS:
        across(t).start()
    along(0, lag_send.at[me_w])
    for t in HOPS[::-1]:
        across(t).wait_recv()
        along(t, lag_held.at[t])

    counts = []
    for j in range(PC // N_WIN):
        count = jnp.zeros((PR, 128), f32)
        for w in range(N_WIN):
            column = pl.ds(NEED * w + PR + (PC // N_WIN) * me_w + j, 1)
            count = count + final_present[NEED * w : NEED * w + PR, :] * final_present[column, :]
        counts.append(count)
    count = jnp.maximum(jnp.concatenate(counts, axis=0)[:, :1], 1.0)

    total = jnp.zeros((SHARE, LAGS), f32)
    for k in range(NZ):
        piece = lag_recv.at[k]
        pltpu.make_async_copy(piece, piece, f_recv.at[k]).wait()
        total = total + lag_recv[k].astype(f32)
    out_ref[...] = total / count

    for s in range(STEPS):
        sent = recv1.at[s, pl.ds(0, NZ - 1)]
        pltpu.make_async_copy(sent, sent, d_send.at[s]).wait()
        sent = send2.at[s, pl.ds(0, PLANE - 1)]
        pltpu.make_async_copy(sent, sent, s_send.at[s]).wait()
    pltpu.make_async_copy(near_masks, near_masks, m_send.at[0]).wait()
    pltpu.make_async_copy(far_masks, far_masks, m_send.at[1]).wait()
    for t in range(1, N_WIN):
        across(t).wait_send()
    for t in range(N_WIN):

        @pl.when((me_w - t + N_WIN) % N_WIN != z)
        def _(t=t):
            along_remote(t, lag_send.at[0]).wait_send()


def per_device(spectra, availability, owners):
    dma = pltpu.SemaphoreType.DMA
    anywhere = pl.BlockSpec(memory_space=pl.ANY)
    out = pl.pallas_call(
        kernel,
        out_shape=jax.ShapeDtypeStruct((SHARE, LAGS), f32),
        in_specs=[anywhere] * 3,
        out_specs=pl.BlockSpec(memory_space=pltpu.VMEM),
        scratch_shapes=[
            pltpu.VMEM((BLOCK, 2, BINS), bf16),
            pltpu.VMEM((N_PAIR, NEED), i32),
            pltpu.VMEM((1, BLOCK), i32),
            pltpu.VMEM((STEPS, NZ, BLOCK, 2, SUB), bf16),
            pltpu.VMEM((STEPS, N_PAIR, MSG, SUB), bf16),
            pltpu.VMEM((STEPS, PLANE, MSG, SUB), bf16),
            pltpu.VMEM((STEPS, 2 * SUB, LAGS), bf16),
            pltpu.VMEM((N_WIN, 2, NEED, SUB), f32),
            pltpu.VMEM((2 * PAIRS, 2 * SUB), bf16),
            pltpu.VMEM((PAIRS, LAGS), f32),
            pltpu.VMEM((HALVES, 16 * N_PAIR, QUAD * 2 * BLOCK), bf16),
            pltpu.VMEM((CHUNK // FINE, LAGS), f32),
            pltpu.VMEM((CHUNK // FINE, LAGS), f32),
            pltpu.VMEM((NZ, 1, 128), f32),
            pltpu.VMEM((N_WIN * N_PAIR, 1, 128), f32),
            pltpu.VMEM((N_WIN * NEED, 128), f32),
            pltpu.VMEM((N_WIN * NEED, 128), f32),
            pltpu.VMEM((N_WIN, SHARE, LAGS), bf16),
            pltpu.VMEM((N_WIN, SHARE, LAGS), bf16),
            pltpu.VMEM((NZ, SHARE, LAGS), bf16),
            dma((3,)),
            dma((STEPS,)),
            dma((STEPS,)),
            dma((STEPS,)),
            dma((STEPS,)),
            dma((2,)),
            dma((2,)),
            dma((N_WIN,)),
            dma((N_WIN,)),
            dma((N_WIN,)),
            dma((NZ,)),
        ],
        compiler_params=pltpu.CompilerParams(
            collective_id=0, has_side_effects=True, vmem_limit_bytes=48 * 1024 * 1024
        ),
        cost_estimate=pl.CostEstimate(
            flops=6_000_000_000, bytes_accessed=2_000_000, transcendentals=1_000_000
        ),
    )(spectra, owners, availability)
    return out.reshape(PC // N_WIN, PR, LAGS)


def solution(mesh):
    return jax.shard_map(
        per_device,
        mesh=mesh,
        in_specs=(P("win", "pair", None, None), P("win", "pair"), P()),
        out_specs=P("win", "pair", None),
        check_vma=False,
    )
```

```python
import math

import jax
import jax.numpy as jnp
from jax import lax
from jax.experimental import pallas as pl
from jax.experimental.pallas import tpu as pltpu
from jax.sharding import PartitionSpec as P

WB = 64
LAGS = 512
PR = 16
PC = 16
NEED = 32
EPSILON = 1e-06

NX, NZ = 4, 8
N_PAIR = NX * NZ
N_WIN = 8
BLOCK = 32
BINS = 8192
CHUNK = BINS // NZ
WIDTHS = (256, 256, 256, 256)
STEPS = len(WIDTHS)
STARTS = tuple(sum(WIDTHS[:s]) for s in range(STEPS))
WIDEST = max(WIDTHS)
AHEAD = 2
PLANE = NX * N_WIN
HALVES = 2
QUAD = NZ // HALVES
MSG = 4 * NZ
PERIOD = 2 * BINS
FINE = 32
PAIRS = PC * PR
SHARE = PAIRS // N_WIN

f32 = jnp.float32
bf16 = jnp.bfloat16
i32 = jnp.int32

Z_OFFSETS = [4, 3, -3, 2, -2, 1, -1]
PLANE_OFFSETS = [(dw, dx) for dw in (4, 3, 5, 2, 6, 1, 7, 0) for dx in (2, 1, -1, 0)][:-1]


def iota(shape, dim):
    return lax.broadcasted_iota(i32, shape, dim)


def work_z(w, z):
    y, core = w // 2, w % 2
    near = jnp.where(y < 2, 4 - 2 * y, 3 - 2 * ((y + z) % 2))
    return (z + near + 4 * core) % NZ


def worker(offset, z):
    core = 0 if 1 <= offset <= 4 else 1
    near = offset - 4 * core
    near = near + NZ if near < 0 else near
    odd = z % 2
    y = {4: 0, 2: 1, 3: 2 + odd, 1: 3 - odd}[near]
    return 2 * y + core


def kernel(
    x_hbm,
    own_hbm,
    avail_hbm,
    out_ref,
    x_ref,
    own_ref,
    avail_ref,
    white,
    lhs,
    acc,
    smat,
    cos_a,
    sin_a,
    mask_z,
    mask_all,
    present,
    final_present,
    lag_send,
    lag_recv,
    in_sem,
    d_send,
    d_recv,
    s_send,
    s_recv,
    m_send,
    m_recv,
    l_send,
    l_recv,
    *steps,
):
    recv1, send2, recv2, table = (steps[STEPS * i : STEPS * (i + 1)] for i in range(4))
    me_w = lax.axis_index("win")
    me_p = lax.axis_index("pair")
    x, z = me_p // NZ, me_p % NZ
    z_peers = [(z + dz + NZ) % NZ for dz in Z_OFFSETS]
    my_owner_z = work_z(me_w, z)
    plane_peers = [((me_w + dw) % N_WIN, (x + dx + NX) % NX) for dw, dx in PLANE_OFFSETS]

    barrier = pltpu.get_barrier_semaphore()
    for k in z_peers:
        pl.semaphore_signal(barrier, inc=1, device_id={"pair": x * NZ + k})
    for o, k in plane_peers:
        pl.semaphore_signal(barrier, inc=1, device_id={"win": o, "pair": k * NZ + z})
    for offset in range(1, NZ):
        k = (z - offset + NZ) % NZ
        pl.semaphore_signal(
            barrier, inc=1, device_id={"win": worker(offset, k), "pair": x * NZ + k}
        )
    own_in = pltpu.make_async_copy(own_hbm, own_ref, in_sem.at[0])
    avail_in = pltpu.make_async_copy(avail_hbm, avail_ref, in_sem.at[1])
    x_in = pltpu.make_async_copy(x_hbm.at[0], x_ref, in_sem.at[2])
    own_in.start()
    avail_in.start()
    x_in.start()
    avail_in.wait()
    mask_z[z] = jnp.concatenate(
        [avail_ref[...].astype(f32), jnp.zeros((1, 128 - BLOCK), f32)], axis=1
    )
    x_in.wait()
    pl.semaphore_wait(barrier, NZ - 1 + PLANE - 1 + jnp.where(me_w == 1, 0, N_WIN))


    def spectra_step(s, k):
        bins = pl.ds(pl.multiple_of(k * CHUNK + STARTS[s], 128), WIDTHS[s])
        return x_ref.at[:, :, bins]

    def start_spectra(s):
        for k in z_peers:
            pltpu.make_async_remote_copy(
                src_ref=spectra_step(s, k),
                dst_ref=recv1[s].at[z],
                send_sem=d_send.at[s],
                recv_sem=d_recv.at[s],
                device_id={"pair": x * NZ + k},
            ).start()
        pltpu.make_async_copy(spectra_step(s, z), recv1[s].at[z], d_recv.at[s]).start()

    for k in z_peers:
        pltpu.make_async_remote_copy(
            src_ref=mask_z.at[z],
            dst_ref=mask_z.at[z],
            send_sem=m_send.at[0],
            recv_sem=m_recv.at[0],
            device_id={"pair": x * NZ + k},
        ).start()

    for s in range(AHEAD):
        start_spectra(s)
    own_in.wait()

    rows = 16 * N_PAIR
    owners = own_ref[...]
    spread = (iota((rows, N_PAIR), 0) >> 4 == iota((rows, N_PAIR), 1)).astype(bf16)
    block = jnp.dot(spread, (owners >> 5).astype(bf16), preferred_element_type=f32)
    station = jnp.dot(spread, (owners & 31).astype(bf16), preferred_element_type=f32)
    row = iota((rows, 1), 0)
    near = (row >> 2) & 3
    upper_slot = ((row >> 1) & 1) == 1
    for half in range(HALVES):
        mine = block == (x * NZ + half * QUAD + near).astype(f32)
        first = jnp.min(jnp.where(mine, station, BLOCK - 1.0), axis=1, keepdims=True)
        last = jnp.max(jnp.where(mine, station, 0.0), axis=1, keepdims=True)
        wanted = jnp.where(upper_slot, last, first).astype(i32)
        source = near * (2 * BLOCK) + 2 * wanted + (row & 1)
        smat[half] = (iota((rows, QUAD * 2 * BLOCK), 1) == source).astype(bf16)

    near_masks = mask_z.at[pl.ds(0, NZ - 1)]
    pltpu.make_async_copy(near_masks, near_masks, m_recv.at[0]).wait()
    here = pl.ds((me_w * NX + x) * NZ, NZ)
    for o, k in plane_peers:
        pltpu.make_async_remote_copy(
            src_ref=mask_z,
            dst_ref=mask_all.at[here],
            send_sem=m_send.at[1],
            recv_sem=m_recv.at[1],
            device_id={"win": o, "pair": k * NZ + z},
        ).start()
    mask_all[here] = mask_z[...]
    far_masks = mask_all.at[pl.ds(0, N_WIN * N_PAIR - NZ)]

    def relay(s):
        whole = recv1[s]
        pltpu.make_async_copy(whole, whole, d_recv.at[s]).wait()

        if s + AHEAD < STEPS:
            start_spectra(s + AHEAD)

        for half in range(HALVES):
            stations = recv1[s][half * QUAD : (half + 1) * QUAD]
            stations = stations.reshape(QUAD * 2 * BLOCK, WIDTHS[s])
            message = jnp.dot(smat[half], stations, preferred_element_type=f32).astype(bf16)
            send2[s][:, 16 * half : 16 * (half + 1), :] = message.reshape(N_PAIR, 16, WIDTHS[s])
        for o, k in plane_peers:
            pltpu.make_async_remote_copy(
                src_ref=send2[s].at[k * NZ + work_z(o, z)],
                dst_ref=recv2[s].at[me_w * NX + x],
                send_sem=s_send.at[s],
                recv_sem=s_recv.at[s],
                device_id={"win": o, "pair": k * NZ + z},
            ).start()
        recv2[s][me_w * NX + x] = send2[s][x * NZ + my_owner_z]

    def process(s):
        wide = WIDTHS[s]
        others = recv2[s].at[pl.ds(0, PLANE - 1)]
        pltpu.make_async_copy(others, others, s_recv.at[s]).wait()
        for w in range(N_WIN):
            messages = recv2[s][NX * w : NX * (w + 1)].reshape(NX * MSG, wide)
            lines = jnp.dot(rmat, messages, preferred_element_type=f32)
            re, im = lines[:NEED], lines[NEED:]
            magnitude = jnp.sqrt(re * re + im * im)
            upper = magnitude.astype(bf16)
            lower = (magnitude - upper.astype(f32)).astype(bf16)
            level = jnp.dot(upper, band[:wide, :wide], preferred_element_type=f32) + jnp.dot(
                lower, band[:wide, :wide], preferred_element_type=f32
            )
            factor = present[NEED * w : NEED * (w + 1), :1] / (level + EPSILON)
            white[w, 0, :, :wide] = (re * factor).astype(bf16).astype(f32)
            white[w, 1, :, :wide] = (im * factor).astype(bf16).astype(f32)
        for j in range(PC):
            total_re = jnp.zeros((PR, wide), f32)
            total_im = jnp.zeros((PR, wide), f32)
            for w in range(N_WIN):
                ar, ai = white[w, 0, :PR, :wide], white[w, 1, :PR, :wide]
                br = white[w, 0, PR + j : PR + j + 1, :wide]
                bi = white[w, 1, PR + j : PR + j + 1, :wide]
                total_re = total_re + (ar * br + ai * bi)
                total_im = total_im + (ai * br - ar * bi)
            for part, total in enumerate((total_re, total_im)):
                upper = total.astype(bf16)
                lower = (total - upper.astype(f32)).astype(bf16)
                lhs[PR * j : PR * (j + 1), wide * part : wide * (part + 1)] = upper
                lhs[PAIRS + PR * j : PAIRS + PR * (j + 1), wide * part : wide * (part + 1)] = lower
        product = jnp.dot(lhs[:, : 2 * wide], table[s][...], preferred_element_type=f32)
        acc[...] += product[:PAIRS] + product[PAIRS:]

    relay(0)

    lag = iota((FINE, LAGS), 1) - LAGS // 2
    index = iota((FINE, LAGS), 0)

    def angle(phase):
        phase = ((phase + PERIOD // 2) & (PERIOD - 1)) - PERIOD // 2
        return phase.astype(f32) * (2.0 * math.pi / PERIOD)

    coarse = angle((z * CHUNK + FINE * index) * lag)
    cos_a[...] = jnp.cos(coarse)
    sin_a[...] = jnp.sin(coarse)
    fine = angle(index * lag)
    cos_b, sin_b = jnp.cos(fine), jnp.sin(fine)

    for s in range(STEPS):

        def table_rows(n, carry, s=s):
            at = STARTS[s] // FINE + n
            ca, sa = cos_a[pl.ds(at, 1), :], sin_a[pl.ds(at, 1), :]
            bins = z * CHUNK + FINE * at + iota((FINE, 1), 0)
            weight = jnp.where(bins == 0, 1.0, 2.0) / math.sqrt(PERIOD)
            real = pl.ds(pl.multiple_of(n * FINE, FINE), FINE)
            imag = pl.ds(pl.multiple_of(WIDTHS[s] + n * FINE, FINE), FINE)
            table[s][real, :] = (weight * (ca * cos_b - sa * sin_b)).astype(bf16)
            table[s][imag, :] = (-weight * (sa * cos_b + ca * sin_b)).astype(bf16)
            return carry

        lax.fori_loop(0, WIDTHS[s] // FINE, table_rows, 0)

    def pick(count, lane, own_row):
        hit = iota((count, NEED), 1) == lane
        return jnp.sum(jnp.where(hit, own_row, 0), axis=1, keepdims=True)

    work_row = own_ref[pl.ds(x * NZ + my_owner_z, 1), :]
    sel = iota((2 * NEED, 1), 0)
    chosen = pick(2 * NEED, sel & (NEED - 1), work_row)
    earlier = jnp.logical_and(work_row >> 5 == chosen >> 5, work_row < chosen)
    slot = jnp.max(earlier.astype(f32), axis=1, keepdims=True).astype(i32)
    target = (chosen >> 5) * 4 + slot * 2 + (sel >> 5)
    rmat = (iota((2 * NEED, NX * MSG), 1) == target).astype(bf16)
    band = jnp.where(iota((WIDEST, WIDEST), 0) >> 6 == iota((WIDEST, WIDEST), 1) >> 6, 1.0 / WB, 0.0)
    band = band.astype(bf16)
    acc[...] = jnp.zeros_like(acc)

    line = iota((N_WIN * NEED, 1), 0)

    def availability_of(masks, own_row):
        who = pick(N_WIN * NEED, line & (NEED - 1), own_row)
        place = (line >> 5) * N_PAIR + (who >> 5)
        where = (iota((N_WIN * NEED, N_WIN * N_PAIR), 1) == place).astype(bf16)
        found = jnp.dot(where, masks, preferred_element_type=f32)
        hit = iota((N_WIN * NEED, 128), 1) == who & 31
        value = jnp.sum(jnp.where(hit, found, 0.0), axis=1, keepdims=True)
        return jnp.broadcast_to(value, (N_WIN * NEED, 128))


    relay(1)
    pltpu.make_async_copy(far_masks, far_masks, m_recv.at[1]).wait()
    masks = mask_all[:, 0, :].astype(bf16)
    present[...] = availability_of(masks, work_row)
    final_present[...] = availability_of(masks, own_ref[pl.ds(me_p, 1), :])
    process(0)
    for s in range(2, STEPS):
        relay(s)
        process(s - 1)
    process(STEPS - 1)

    lag_send[...] = acc[...].astype(bf16).reshape(N_WIN, SHARE, LAGS)

    def lagged(t):
        o = (me_w + t) % N_WIN
        return pltpu.make_async_remote_copy(
            src_ref=lag_send.at[o],
            dst_ref=lag_recv.at[z],
            send_sem=l_send.at[t],
            recv_sem=l_recv.at[z],
            device_id={"win": o, "pair": x * NZ + my_owner_z},
        )

    for t in (4, 3, 5, 2, 6, 1, 7):
        lagged(t).start()

    @pl.when(me_w == 1)
    def _():
        pltpu.make_async_copy(lag_send.at[me_w], lag_recv.at[z], l_recv.at[z]).start()

    @pl.when(me_w != 1)
    def _():
        lagged(0).start()

    counts = []
    for j in range(PC // N_WIN):
        count = jnp.zeros((PR, 128), f32)
        for w in range(N_WIN):
            column = pl.ds(NEED * w + PR + (PC // N_WIN) * me_w + j, 1)
            count = count + final_present[NEED * w : NEED * w + PR, :] * final_present[column, :]
        counts.append(count)
    count = jnp.maximum(jnp.concatenate(counts, axis=0)[:, :1], 1.0)

    total = jnp.zeros((SHARE, LAGS), f32)
    for k in range(NZ):
        piece = lag_recv.at[k]
        pltpu.make_async_copy(piece, piece, l_recv.at[k]).wait()
        total = total + lag_recv[k].astype(f32)
    out_ref[...] = total / count

    for s in range(STEPS):
        sent = recv1[s].at[pl.ds(0, NZ - 1)]
        pltpu.make_async_copy(sent, sent, d_send.at[s]).wait()
        sent = send2[s].at[pl.ds(0, PLANE - 1)]
        pltpu.make_async_copy(sent, sent, s_send.at[s]).wait()
    pltpu.make_async_copy(near_masks, near_masks, m_send.at[0]).wait()
    pltpu.make_async_copy(far_masks, far_masks, m_send.at[1]).wait()
    for t in range(1, N_WIN):
        lagged(t).wait_send()

    @pl.when(me_w != 1)
    def _():
        lagged(0).wait_send()


def per_device(spectra, availability, owners):
    dma = pltpu.SemaphoreType.DMA
    anywhere = pl.BlockSpec(memory_space=pl.ANY)
    out = pl.pallas_call(
        kernel,
        out_shape=jax.ShapeDtypeStruct((SHARE, LAGS), f32),
        in_specs=[anywhere] * 3,
        out_specs=pl.BlockSpec(memory_space=pltpu.VMEM),
        scratch_shapes=[
            pltpu.VMEM((BLOCK, 2, BINS), bf16),
            pltpu.VMEM((N_PAIR, NEED), i32),
            pltpu.VMEM((1, BLOCK), i32),
            pltpu.VMEM((N_WIN, 2, NEED, WIDEST), f32),
            pltpu.VMEM((2 * PAIRS, 2 * WIDEST), bf16),
            pltpu.VMEM((PAIRS, LAGS), f32),
            pltpu.VMEM((HALVES, 16 * N_PAIR, QUAD * 2 * BLOCK), bf16),
            pltpu.VMEM((CHUNK // FINE, LAGS), f32),
            pltpu.VMEM((CHUNK // FINE, LAGS), f32),
            pltpu.VMEM((NZ, 1, 128), f32),
            pltpu.VMEM((N_WIN * N_PAIR, 1, 128), f32),
            pltpu.VMEM((N_WIN * NEED, 128), f32),
            pltpu.VMEM((N_WIN * NEED, 128), f32),
            pltpu.VMEM((N_WIN, SHARE, LAGS), bf16),
            pltpu.VMEM((NZ, SHARE, LAGS), bf16),
            dma((3,)),
            dma((STEPS,)),
            dma((STEPS,)),
            dma((STEPS,)),
            dma((STEPS,)),
            dma((2,)),
            dma((2,)),
            dma((N_WIN,)),
            dma((NZ,)),
        ]
        + [pltpu.VMEM((NZ, BLOCK, 2, wide), bf16) for wide in WIDTHS]
        + [pltpu.VMEM((N_PAIR, MSG, wide), bf16) for wide in WIDTHS]
        + [pltpu.VMEM((PLANE, MSG, wide), bf16) for wide in WIDTHS]
        + [pltpu.VMEM((2 * wide, LAGS), bf16) for wide in WIDTHS],
        compiler_params=pltpu.CompilerParams(
            collective_id=0, has_side_effects=True, vmem_limit_bytes=48 * 1024 * 1024
        ),
        cost_estimate=pl.CostEstimate(
            flops=6_000_000_000, bytes_accessed=2_000_000, transcendentals=1_000_000
        ),
    )(spectra, owners, availability)
    return out.reshape(PC // N_WIN, PR, LAGS)


def solution(mesh):
    return jax.shard_map(
        per_device,
        mesh=mesh,
        in_specs=(P("win", "pair", None, None), P("win", "pair"), P()),
        out_specs=P("win", "pair", None),
        check_vma=False,
    )
```

```python
import math

import jax
import jax.numpy as jnp
from jax import lax
from jax.experimental import pallas as pl
from jax.experimental.pallas import tpu as pltpu
from jax.sharding import PartitionSpec as P

WB = 64
LAGS = 512
PR = 16
PC = 16
NEED = 32
EPSILON = 1e-06

NX, NZ = 4, 8
N_PAIR = NX * NZ
N_WIN = 8
BLOCK = 32
BINS = 8192
CHUNK = BINS // NZ
WIDTHS = (128,) * 8
STEPS = len(WIDTHS)
STARTS = tuple(sum(WIDTHS[:s]) for s in range(STEPS))
WIDEST = max(WIDTHS)
AHEAD = 3
PLANE = NX * N_WIN
HALVES = 2
QUAD = NZ // HALVES
MSG = 4 * NZ
PERIOD = 2 * BINS
FINE = 32
PAIRS = PC * PR
SHARE = PAIRS // N_WIN

f32 = jnp.float32
bf16 = jnp.bfloat16
i32 = jnp.int32

Z_OFFSETS = [4, 3, -3, 2, -2, 1, -1]
PLANE_OFFSETS = [(dw, dx) for dw in (4, 3, 5, 2, 6, 1, 7, 0) for dx in (2, 1, -1, 0)][:-1]


def iota(shape, dim):
    return lax.broadcasted_iota(i32, shape, dim)


def work_z(w, z):
    y, core = w // 2, w % 2
    near = jnp.where(y < 2, 4 - 2 * y, 3 - 2 * ((y + z) % 2))
    return (z + near + 4 * core) % NZ


def worker(offset, z):
    core = 0 if 1 <= offset <= 4 else 1
    near = offset - 4 * core
    near = near + NZ if near < 0 else near
    odd = z % 2
    y = {4: 0, 2: 1, 3: 2 + odd, 1: 3 - odd}[near]
    return 2 * y + core


def kernel(
    x_hbm,
    own_hbm,
    avail_hbm,
    out_ref,
    x_ref,
    own_ref,
    avail_ref,
    white,
    lhs,
    acc,
    smat,
    cos_a,
    sin_a,
    mask_z,
    mask_all,
    present,
    final_present,
    lag_send,
    lag_recv,
    in_sem,
    d_send,
    d_recv,
    s_send,
    s_recv,
    m_send,
    m_recv,
    l_send,
    l_recv,
    *steps,
):
    recv1, send2, recv2, table = (steps[STEPS * i : STEPS * (i + 1)] for i in range(4))
    me_w = lax.axis_index("win")
    me_p = lax.axis_index("pair")
    x, z = me_p // NZ, me_p % NZ
    z_peers = [(z + dz + NZ) % NZ for dz in Z_OFFSETS]
    my_owner_z = work_z(me_w, z)
    plane_peers = [((me_w + dw) % N_WIN, (x + dx + NX) % NX) for dw, dx in PLANE_OFFSETS]

    barrier = pltpu.get_barrier_semaphore()
    for k in z_peers:
        pl.semaphore_signal(barrier, inc=1, device_id={"pair": x * NZ + k})
    for o, k in plane_peers:
        pl.semaphore_signal(barrier, inc=1, device_id={"win": o, "pair": k * NZ + z})
    for offset in range(1, NZ):
        k = (z - offset + NZ) % NZ
        pl.semaphore_signal(
            barrier, inc=1, device_id={"win": worker(offset, k), "pair": x * NZ + k}
        )
    own_in = pltpu.make_async_copy(own_hbm, own_ref, in_sem.at[0])
    avail_in = pltpu.make_async_copy(avail_hbm, avail_ref, in_sem.at[1])
    x_in = pltpu.make_async_copy(x_hbm.at[0], x_ref, in_sem.at[2])
    own_in.start()
    avail_in.start()
    x_in.start()
    avail_in.wait()
    mask_z[z] = jnp.concatenate(
        [avail_ref[...].astype(f32), jnp.zeros((1, 128 - BLOCK), f32)], axis=1
    )
    x_in.wait()
    pl.semaphore_wait(barrier, NZ - 1 + PLANE - 1 + jnp.where(me_w == 1, 0, N_WIN))


    def spectra_step(s, k):
        bins = pl.ds(pl.multiple_of(k * CHUNK + STARTS[s], 128), WIDTHS[s])
        return x_ref.at[:, :, bins]

    def start_spectra(s):
        for k in z_peers:
            pltpu.make_async_remote_copy(
                src_ref=spectra_step(s, k),
                dst_ref=recv1[s].at[z],
                send_sem=d_send.at[s],
                recv_sem=d_recv.at[s],
                device_id={"pair": x * NZ + k},
            ).start()
        pltpu.make_async_copy(spectra_step(s, z), recv1[s].at[z], d_recv.at[s]).start()

    for k in z_peers:
        pltpu.make_async_remote_copy(
            src_ref=mask_z.at[z],
            dst_ref=mask_z.at[z],
            send_sem=m_send.at[0],
            recv_sem=m_recv.at[0],
            device_id={"pair": x * NZ + k},
        ).start()

    for s in range(AHEAD):
        start_spectra(s)
    own_in.wait()

    rows = 16 * N_PAIR
    owners = own_ref[...]
    spread = (iota((rows, N_PAIR), 0) >> 4 == iota((rows, N_PAIR), 1)).astype(bf16)
    block = jnp.dot(spread, (owners >> 5).astype(bf16), preferred_element_type=f32)
    station = jnp.dot(spread, (owners & 31).astype(bf16), preferred_element_type=f32)
    row = iota((rows, 1), 0)
    near = (row >> 2) & 3
    upper_slot = ((row >> 1) & 1) == 1
    for half in range(HALVES):
        mine = block == (x * NZ + half * QUAD + near).astype(f32)
        first = jnp.min(jnp.where(mine, station, BLOCK - 1.0), axis=1, keepdims=True)
        last = jnp.max(jnp.where(mine, station, 0.0), axis=1, keepdims=True)
        wanted = jnp.where(upper_slot, last, first).astype(i32)
        source = near * (2 * BLOCK) + 2 * wanted + (row & 1)
        smat[half] = (iota((rows, QUAD * 2 * BLOCK), 1) == source).astype(bf16)

    near_masks = mask_z.at[pl.ds(0, NZ - 1)]
    pltpu.make_async_copy(near_masks, near_masks, m_recv.at[0]).wait()
    here = pl.ds((me_w * NX + x) * NZ, NZ)
    for o, k in plane_peers:
        pltpu.make_async_remote_copy(
            src_ref=mask_z,
            dst_ref=mask_all.at[here],
            send_sem=m_send.at[1],
            recv_sem=m_recv.at[1],
            device_id={"win": o, "pair": k * NZ + z},
        ).start()
    mask_all[here] = mask_z[...]
    far_masks = mask_all.at[pl.ds(0, N_WIN * N_PAIR - NZ)]

    def relay(s):
        whole = recv1[s]
        pltpu.make_async_copy(whole, whole, d_recv.at[s]).wait()

        if s + AHEAD < STEPS:
            start_spectra(s + AHEAD)

        for half in range(HALVES):
            stations = recv1[s][half * QUAD : (half + 1) * QUAD]
            stations = stations.reshape(QUAD * 2 * BLOCK, WIDTHS[s])
            message = jnp.dot(smat[half], stations, preferred_element_type=f32).astype(bf16)
            send2[s][:, 16 * half : 16 * (half + 1), :] = message.reshape(N_PAIR, 16, WIDTHS[s])
        for o, k in plane_peers:
            pltpu.make_async_remote_copy(
                src_ref=send2[s].at[k * NZ + work_z(o, z)],
                dst_ref=recv2[s].at[me_w * NX + x],
                send_sem=s_send.at[s],
                recv_sem=s_recv.at[s],
                device_id={"win": o, "pair": k * NZ + z},
            ).start()
        recv2[s][me_w * NX + x] = send2[s][x * NZ + my_owner_z]

    def process(s):
        wide = WIDTHS[s]
        others = recv2[s].at[pl.ds(0, PLANE - 1)]
        pltpu.make_async_copy(others, others, s_recv.at[s]).wait()
        res, ims, magnitudes = [], [], []
        for w in range(N_WIN):
            messages = recv2[s][NX * w : NX * (w + 1)].reshape(NX * MSG, wide)
            lines = jnp.dot(rmat, messages, preferred_element_type=f32)
            res.append(lines[:NEED])
            ims.append(lines[NEED:])
            magnitudes.append(jnp.sqrt(res[w] * res[w] + ims[w] * ims[w]))
        magnitude = jnp.concatenate(magnitudes, axis=0)
        upper = magnitude.astype(bf16)
        lower = (magnitude - upper.astype(f32)).astype(bf16)
        both = jnp.concatenate([upper, lower], axis=0)
        levels = jnp.dot(both, band[:wide, :wide], preferred_element_type=f32)
        level = levels[: N_WIN * NEED] + levels[N_WIN * NEED :]
        factor = present[:, :1] / (level + EPSILON)
        for w in range(N_WIN):
            own = factor[NEED * w : NEED * (w + 1)]
            white[w, 0, :, :wide] = (res[w] * own).astype(bf16).astype(f32)
            white[w, 1, :, :wide] = (ims[w] * own).astype(bf16).astype(f32)
        for j in range(PC):
            total_re = jnp.zeros((PR, wide), f32)
            total_im = jnp.zeros((PR, wide), f32)
            for w in range(N_WIN):
                ar, ai = white[w, 0, :PR, :wide], white[w, 1, :PR, :wide]
                br = white[w, 0, PR + j : PR + j + 1, :wide]
                bi = white[w, 1, PR + j : PR + j + 1, :wide]
                total_re = total_re + (ar * br + ai * bi)
                total_im = total_im + (ai * br - ar * bi)
            for part, total in enumerate((total_re, total_im)):
                upper = total.astype(bf16)
                lower = (total - upper.astype(f32)).astype(bf16)
                lhs[PR * j : PR * (j + 1), wide * part : wide * (part + 1)] = upper
                lhs[PAIRS + PR * j : PAIRS + PR * (j + 1), wide * part : wide * (part + 1)] = lower
        product = jnp.dot(lhs[:, : 2 * wide], table[s][...], preferred_element_type=f32)
        acc[...] += product[:PAIRS] + product[PAIRS:]

    relay(0)

    lag = iota((FINE, LAGS), 1) - LAGS // 2
    index = iota((FINE, LAGS), 0)

    def angle(phase):
        phase = ((phase + PERIOD // 2) & (PERIOD - 1)) - PERIOD // 2
        return phase.astype(f32) * (2.0 * math.pi / PERIOD)

    coarse = angle((z * CHUNK + FINE * index) * lag)
    cos_a[...] = jnp.cos(coarse)
    sin_a[...] = jnp.sin(coarse)
    fine = angle(index * lag)
    cos_b, sin_b = jnp.cos(fine), jnp.sin(fine)

    for s in range(STEPS):

        def table_rows(n, carry, s=s):
            at = STARTS[s] // FINE + n
            ca, sa = cos_a[pl.ds(at, 1), :], sin_a[pl.ds(at, 1), :]
            bins = z * CHUNK + FINE * at + iota((FINE, 1), 0)
            weight = jnp.where(bins == 0, 1.0, 2.0) / math.sqrt(PERIOD)
            real = pl.ds(pl.multiple_of(n * FINE, FINE), FINE)
            imag = pl.ds(pl.multiple_of(WIDTHS[s] + n * FINE, FINE), FINE)
            table[s][real, :] = (weight * (ca * cos_b - sa * sin_b)).astype(bf16)
            table[s][imag, :] = (-weight * (sa * cos_b + ca * sin_b)).astype(bf16)
            return carry

        lax.fori_loop(0, WIDTHS[s] // FINE, table_rows, 0)

    def pick(count, lane, own_row):
        hit = iota((count, NEED), 1) == lane
        return jnp.sum(jnp.where(hit, own_row, 0), axis=1, keepdims=True)

    work_row = own_ref[pl.ds(x * NZ + my_owner_z, 1), :]
    sel = iota((2 * NEED, 1), 0)
    chosen = pick(2 * NEED, sel & (NEED - 1), work_row)
    earlier = jnp.logical_and(work_row >> 5 == chosen >> 5, work_row < chosen)
    slot = jnp.max(earlier.astype(f32), axis=1, keepdims=True).astype(i32)
    target = (chosen >> 5) * 4 + slot * 2 + (sel >> 5)
    rmat = (iota((2 * NEED, NX * MSG), 1) == target).astype(bf16)
    band = jnp.where(iota((WIDEST, WIDEST), 0) >> 6 == iota((WIDEST, WIDEST), 1) >> 6, 1.0 / WB, 0.0)
    band = band.astype(bf16)
    acc[...] = jnp.zeros_like(acc)

    line = iota((N_WIN * NEED, 1), 0)

    def availability_of(masks, own_row):
        who = pick(N_WIN * NEED, line & (NEED - 1), own_row)
        place = (line >> 5) * N_PAIR + (who >> 5)
        where = (iota((N_WIN * NEED, N_WIN * N_PAIR), 1) == place).astype(bf16)
        found = jnp.dot(where, masks, preferred_element_type=f32)
        hit = iota((N_WIN * NEED, 128), 1) == who & 31
        value = jnp.sum(jnp.where(hit, found, 0.0), axis=1, keepdims=True)
        return jnp.broadcast_to(value, (N_WIN * NEED, 128))


    relay(1)
    pltpu.make_async_copy(far_masks, far_masks, m_recv.at[1]).wait()
    masks = mask_all[:, 0, :].astype(bf16)
    present[...] = availability_of(masks, work_row)
    final_present[...] = availability_of(masks, own_ref[pl.ds(me_p, 1), :])
    for s in range(2, STEPS):
        relay(s)
        process(s - 2)
    for s in range(STEPS - 2, STEPS):
        process(s)

    lag_send[...] = acc[...].astype(bf16).reshape(N_WIN, SHARE, LAGS)

    def lagged(t):
        o = (me_w + t) % N_WIN
        return pltpu.make_async_remote_copy(
            src_ref=lag_send.at[o],
            dst_ref=lag_recv.at[z],
            send_sem=l_send.at[t],
            recv_sem=l_recv.at[z],
            device_id={"win": o, "pair": x * NZ + my_owner_z},
        )

    for t in (4, 3, 5, 2, 6, 1, 7):
        lagged(t).start()

    @pl.when(me_w == 1)
    def _():
        pltpu.make_async_copy(lag_send.at[me_w], lag_recv.at[z], l_recv.at[z]).start()

    @pl.when(me_w != 1)
    def _():
        lagged(0).start()

    counts = []
    for j in range(PC // N_WIN):
        count = jnp.zeros((PR, 128), f32)
        for w in range(N_WIN):
            column = pl.ds(NEED * w + PR + (PC // N_WIN) * me_w + j, 1)
            count = count + final_present[NEED * w : NEED * w + PR, :] * final_present[column, :]
        counts.append(count)
    count = jnp.maximum(jnp.concatenate(counts, axis=0)[:, :1], 1.0)

    total = jnp.zeros((SHARE, LAGS), f32)
    for k in range(NZ):
        piece = lag_recv.at[k]
        pltpu.make_async_copy(piece, piece, l_recv.at[k]).wait()
        total = total + lag_recv[k].astype(f32)
    out_ref[...] = total / count

    for s in range(STEPS):
        sent = recv1[s].at[pl.ds(0, NZ - 1)]
        pltpu.make_async_copy(sent, sent, d_send.at[s]).wait()
        sent = send2[s].at[pl.ds(0, PLANE - 1)]
        pltpu.make_async_copy(sent, sent, s_send.at[s]).wait()
    pltpu.make_async_copy(near_masks, near_masks, m_send.at[0]).wait()
    pltpu.make_async_copy(far_masks, far_masks, m_send.at[1]).wait()
    for t in range(1, N_WIN):
        lagged(t).wait_send()

    @pl.when(me_w != 1)
    def _():
        lagged(0).wait_send()


def per_device(spectra, availability, owners):
    dma = pltpu.SemaphoreType.DMA
    anywhere = pl.BlockSpec(memory_space=pl.ANY)
    out = pl.pallas_call(
        kernel,
        out_shape=jax.ShapeDtypeStruct((SHARE, LAGS), f32),
        in_specs=[anywhere] * 3,
        out_specs=pl.BlockSpec(memory_space=pltpu.VMEM),
        scratch_shapes=[
            pltpu.VMEM((BLOCK, 2, BINS), bf16),
            pltpu.VMEM((N_PAIR, NEED), i32),
            pltpu.VMEM((1, BLOCK), i32),
            pltpu.VMEM((N_WIN, 2, NEED, WIDEST), f32),
            pltpu.VMEM((2 * PAIRS, 2 * WIDEST), bf16),
            pltpu.VMEM((PAIRS, LAGS), f32),
            pltpu.VMEM((HALVES, 16 * N_PAIR, QUAD * 2 * BLOCK), bf16),
            pltpu.VMEM((CHUNK // FINE, LAGS), f32),
            pltpu.VMEM((CHUNK // FINE, LAGS), f32),
            pltpu.VMEM((NZ, 1, 128), f32),
            pltpu.VMEM((N_WIN * N_PAIR, 1, 128), f32),
            pltpu.VMEM((N_WIN * NEED, 128), f32),
            pltpu.VMEM((N_WIN * NEED, 128), f32),
            pltpu.VMEM((N_WIN, SHARE, LAGS), bf16),
            pltpu.VMEM((NZ, SHARE, LAGS), bf16),
            dma((3,)),
            dma((STEPS,)),
            dma((STEPS,)),
            dma((STEPS,)),
            dma((STEPS,)),
            dma((2,)),
            dma((2,)),
            dma((N_WIN,)),
            dma((NZ,)),
        ]
        + [pltpu.VMEM((NZ, BLOCK, 2, wide), bf16) for wide in WIDTHS]
        + [pltpu.VMEM((N_PAIR, MSG, wide), bf16) for wide in WIDTHS]
        + [pltpu.VMEM((PLANE, MSG, wide), bf16) for wide in WIDTHS]
        + [pltpu.VMEM((2 * wide, LAGS), bf16) for wide in WIDTHS],
        compiler_params=pltpu.CompilerParams(
            collective_id=0, has_side_effects=True, vmem_limit_bytes=48 * 1024 * 1024
        ),
        cost_estimate=pl.CostEstimate(
            flops=6_000_000_000, bytes_accessed=2_000_000, transcendentals=1_000_000
        ),
    )(spectra, owners, availability)
    return out.reshape(PC // N_WIN, PR, LAGS)


def solution(mesh):
    return jax.shard_map(
        per_device,
        mesh=mesh,
        in_specs=(P("win", "pair", None, None), P("win", "pair"), P()),
        out_specs=P("win", "pair", None),
        check_vma=False,
    )
```

```python
import math

import jax
import jax.numpy as jnp
from jax import lax
from jax.experimental import pallas as pl
from jax.experimental.pallas import tpu as pltpu
from jax.sharding import PartitionSpec as P

WB = 64
LAGS = 512
PR = 16
PC = 16
NEED = 32
EPSILON = 1e-06

NX, NZ = 4, 8
N_PAIR = NX * NZ
N_WIN = 8
BLOCK = 32
BINS = 8192
CHUNK = BINS // NZ
WIDTHS = (128,) * 8
STEPS = len(WIDTHS)
STARTS = tuple(sum(WIDTHS[:s]) for s in range(STEPS))
WIDEST = max(WIDTHS)
AHEAD = 3
PLANE = NX * N_WIN
HALVES = 2
QUAD = NZ // HALVES
MSG = 4 * NZ
PERIOD = 2 * BINS
FINE = 32
PAIRS = PC * PR
SHARE = PAIRS // N_WIN

f32 = jnp.float32
bf16 = jnp.bfloat16
i32 = jnp.int32

Z_OFFSETS = [4, 3, -3, 2, -2, 1, -1]
PLANE_OFFSETS = [(dw, dx) for dw in (4, 3, 5, 2, 6, 1, 7, 0) for dx in (2, 1, -1, 0)][:-1]


def iota(shape, dim):
    return lax.broadcasted_iota(i32, shape, dim)


def work_z(w, z):
    y, core = w // 2, w % 2
    near = jnp.where(y < 2, 4 - 2 * y, 3 - 2 * ((y + z) % 2))
    return (z + near + 4 * core) % NZ


def worker(offset, z):
    core = 0 if 1 <= offset <= 4 else 1
    near = offset - 4 * core
    near = near + NZ if near < 0 else near
    odd = z % 2
    y = {4: 0, 2: 1, 3: 2 + odd, 1: 3 - odd}[near]
    return 2 * y + core


def kernel(
    x_hbm,
    own_hbm,
    avail_hbm,
    out_ref,
    x_ref,
    own_ref,
    avail_ref,
    white,
    lhs,
    acc,
    smat,
    cos_a,
    sin_a,
    mask_z,
    mask_all,
    present,
    final_present,
    lag_send,
    lag_recv,
    in_sem,
    d_send,
    d_recv,
    s_send,
    s_recv,
    m_send,
    m_recv,
    l_send,
    l_recv,
    *steps,
):
    recv1, send2, recv2, table = (steps[STEPS * i : STEPS * (i + 1)] for i in range(4))
    me_w = lax.axis_index("win")
    me_p = lax.axis_index("pair")
    x, z = me_p // NZ, me_p % NZ
    z_peers = [(z + dz + NZ) % NZ for dz in Z_OFFSETS]
    my_owner_z = work_z(me_w, z)
    plane_peers = [((me_w + dw) % N_WIN, (x + dx + NX) % NX) for dw, dx in PLANE_OFFSETS]

    barrier = pltpu.get_barrier_semaphore()
    for k in z_peers:
        pl.semaphore_signal(barrier, inc=1, device_id={"pair": x * NZ + k})
    for o, k in plane_peers:
        pl.semaphore_signal(barrier, inc=1, device_id={"win": o, "pair": k * NZ + z})
    for offset in range(1, NZ):
        k = (z - offset + NZ) % NZ
        pl.semaphore_signal(
            barrier, inc=1, device_id={"win": worker(offset, k), "pair": x * NZ + k}
        )
    own_in = pltpu.make_async_copy(own_hbm, own_ref, in_sem.at[0])
    avail_in = pltpu.make_async_copy(avail_hbm, avail_ref, in_sem.at[1])
    x_in = pltpu.make_async_copy(x_hbm.at[0], x_ref, in_sem.at[2])
    own_in.start()
    avail_in.start()
    x_in.start()
    avail_in.wait()
    mask_z[z] = jnp.concatenate(
        [avail_ref[...].astype(f32), jnp.zeros((1, 128 - BLOCK), f32)], axis=1
    )
    x_in.wait()
    pl.semaphore_wait(barrier, NZ - 1 + PLANE - 1 + jnp.where(me_w == 1, 0, N_WIN))


    def spectra_step(s, k):
        bins = pl.ds(pl.multiple_of(k * CHUNK + STARTS[s], 128), WIDTHS[s])
        return x_ref.at[:, :, bins]

    def start_spectra(s):
        for k in z_peers:
            pltpu.make_async_remote_copy(
                src_ref=spectra_step(s, k),
                dst_ref=recv1[s].at[z],
                send_sem=d_send.at[s],
                recv_sem=d_recv.at[s],
                device_id={"pair": x * NZ + k},
            ).start()
        pltpu.make_async_copy(spectra_step(s, z), recv1[s].at[z], d_recv.at[s]).start()

    for k in z_peers:
        pltpu.make_async_remote_copy(
            src_ref=mask_z.at[z],
            dst_ref=mask_z.at[z],
            send_sem=m_send.at[0],
            recv_sem=m_recv.at[0],
            device_id={"pair": x * NZ + k},
        ).start()

    for s in range(AHEAD):
        start_spectra(s)
    own_in.wait()

    rows = 16 * N_PAIR
    owners = own_ref[...]
    spread = (iota((rows, N_PAIR), 0) >> 4 == iota((rows, N_PAIR), 1)).astype(bf16)
    block = jnp.dot(spread, (owners >> 5).astype(bf16), preferred_element_type=f32)
    station = jnp.dot(spread, (owners & 31).astype(bf16), preferred_element_type=f32)
    row = iota((rows, 1), 0)
    near = (row >> 2) & 3
    upper_slot = ((row >> 1) & 1) == 1
    for half in range(HALVES):
        mine = block == (x * NZ + half * QUAD + near).astype(f32)
        first = jnp.min(jnp.where(mine, station, BLOCK - 1.0), axis=1, keepdims=True)
        last = jnp.max(jnp.where(mine, station, 0.0), axis=1, keepdims=True)
        wanted = jnp.where(upper_slot, last, first).astype(i32)
        source = near * (2 * BLOCK) + 2 * wanted + (row & 1)
        smat[half] = (iota((rows, QUAD * 2 * BLOCK), 1) == source).astype(bf16)

    near_masks = mask_z.at[pl.ds(0, NZ - 1)]
    pltpu.make_async_copy(near_masks, near_masks, m_recv.at[0]).wait()
    here = pl.ds((me_w * NX + x) * NZ, NZ)
    for o, k in plane_peers:
        pltpu.make_async_remote_copy(
            src_ref=mask_z,
            dst_ref=mask_all.at[here],
            send_sem=m_send.at[1],
            recv_sem=m_recv.at[1],
            device_id={"win": o, "pair": k * NZ + z},
        ).start()
    mask_all[here] = mask_z[...]
    far_masks = mask_all.at[pl.ds(0, N_WIN * N_PAIR - NZ)]

    def relay(s):
        whole = recv1[s]
        pltpu.make_async_copy(whole, whole, d_recv.at[s]).wait()

        if s + AHEAD < STEPS:
            start_spectra(s + AHEAD)

        for half in range(HALVES):
            stations = recv1[s][half * QUAD : (half + 1) * QUAD]
            stations = stations.reshape(QUAD * 2 * BLOCK, WIDTHS[s])
            message = jnp.dot(smat[half], stations, preferred_element_type=f32).astype(bf16)
            send2[s][:, 16 * half : 16 * (half + 1), :] = message.reshape(N_PAIR, 16, WIDTHS[s])
        for o, k in plane_peers:
            pltpu.make_async_remote_copy(
                src_ref=send2[s].at[k * NZ + work_z(o, z)],
                dst_ref=recv2[s].at[me_w * NX + x],
                send_sem=s_send.at[s],
                recv_sem=s_recv.at[s],
                device_id={"win": o, "pair": k * NZ + z},
            ).start()
        recv2[s][me_w * NX + x] = send2[s][x * NZ + my_owner_z]

    def process(s):
        wide = WIDTHS[s]
        others = recv2[s].at[pl.ds(0, PLANE - 1)]
        pltpu.make_async_copy(others, others, s_recv.at[s]).wait()
        res, ims, magnitudes = [], [], []
        for w in range(N_WIN):
            messages = recv2[s][NX * w : NX * (w + 1)].reshape(NX * MSG, wide)
            lines = jnp.dot(rmat, messages, preferred_element_type=f32)
            res.append(lines[:NEED])
            ims.append(lines[NEED:])
            magnitudes.append(jnp.sqrt(res[w] * res[w] + ims[w] * ims[w]))
        magnitude = jnp.concatenate(magnitudes, axis=0)
        upper = magnitude.astype(bf16)
        lower = (magnitude - upper.astype(f32)).astype(bf16)
        both = jnp.concatenate([upper, lower], axis=0)
        levels = jnp.dot(both, band[:wide, :wide], preferred_element_type=f32)
        level = levels[: N_WIN * NEED] + levels[N_WIN * NEED :]
        factor = present[:, :1] / (level + EPSILON)
        for w in range(N_WIN):
            own = factor[NEED * w : NEED * (w + 1)]
            white[w, 0, :, :wide] = (res[w] * own).astype(bf16).astype(f32)
            white[w, 1, :, :wide] = (ims[w] * own).astype(bf16).astype(f32)
        for j in range(PC):
            total_re = jnp.zeros((PR, wide), f32)
            total_im = jnp.zeros((PR, wide), f32)
            for w in range(N_WIN):
                ar, ai = white[w, 0, :PR, :wide], white[w, 1, :PR, :wide]
                br = white[w, 0, PR + j : PR + j + 1, :wide]
                bi = white[w, 1, PR + j : PR + j + 1, :wide]
                total_re = total_re + (ar * br + ai * bi)
                total_im = total_im + (ai * br - ar * bi)
            for part, total in enumerate((total_re, total_im)):
                upper = total.astype(bf16)
                lower = (total - upper.astype(f32)).astype(bf16)
                lhs[PR * j : PR * (j + 1), wide * part : wide * (part + 1)] = upper
                lhs[PAIRS + PR * j : PAIRS + PR * (j + 1), wide * part : wide * (part + 1)] = lower
        product = jnp.dot(lhs[:, : 2 * wide], table[s][...], preferred_element_type=f32)
        acc[...] += product[:PAIRS] + product[PAIRS:]

    relay(0)

    lag = iota((FINE, LAGS), 1) - LAGS // 2
    index = iota((FINE, LAGS), 0)

    def angle(phase):
        phase = ((phase + PERIOD // 2) & (PERIOD - 1)) - PERIOD // 2
        return phase.astype(f32) * (2.0 * math.pi / PERIOD)

    coarse = angle((z * CHUNK + FINE * index) * lag)
    cos_a[...] = jnp.cos(coarse)
    sin_a[...] = jnp.sin(coarse)
    fine = angle(index * lag)
    cos_b, sin_b = jnp.cos(fine), jnp.sin(fine)

    for s in range(STEPS):

        def table_rows(n, carry, s=s):
            at = STARTS[s] // FINE + n
            ca, sa = cos_a[pl.ds(at, 1), :], sin_a[pl.ds(at, 1), :]
            bins = z * CHUNK + FINE * at + iota((FINE, 1), 0)
            weight = jnp.where(bins == 0, 1.0, 2.0) / math.sqrt(PERIOD)
            real = pl.ds(pl.multiple_of(n * FINE, FINE), FINE)
            imag = pl.ds(pl.multiple_of(WIDTHS[s] + n * FINE, FINE), FINE)
            table[s][real, :] = (weight * (ca * cos_b - sa * sin_b)).astype(bf16)
            table[s][imag, :] = (-weight * (sa * cos_b + ca * sin_b)).astype(bf16)
            return carry

        lax.fori_loop(0, WIDTHS[s] // FINE, table_rows, 0)

    def pick(count, lane, own_row):
        hit = iota((count, NEED), 1) == lane
        return jnp.sum(jnp.where(hit, own_row, 0), axis=1, keepdims=True)

    work_row = own_ref[pl.ds(x * NZ + my_owner_z, 1), :]
    sel = iota((2 * NEED, 1), 0)
    chosen = pick(2 * NEED, sel & (NEED - 1), work_row)
    earlier = jnp.logical_and(work_row >> 5 == chosen >> 5, work_row < chosen)
    slot = jnp.max(earlier.astype(f32), axis=1, keepdims=True).astype(i32)
    target = (chosen >> 5) * 4 + slot * 2 + (sel >> 5)
    rmat = (iota((2 * NEED, NX * MSG), 1) == target).astype(bf16)
    band = jnp.where(iota((WIDEST, WIDEST), 0) >> 6 == iota((WIDEST, WIDEST), 1) >> 6, 1.0 / WB, 0.0)
    band = band.astype(bf16)
    acc[...] = jnp.zeros_like(acc)

    line = iota((N_WIN * NEED, 1), 0)

    def availability_of(masks, own_row):
        who = pick(N_WIN * NEED, line & (NEED - 1), own_row)
        place = (line >> 5) * N_PAIR + (who >> 5)
        where = (iota((N_WIN * NEED, N_WIN * N_PAIR), 1) == place).astype(bf16)
        found = jnp.dot(where, masks, preferred_element_type=f32)
        hit = iota((N_WIN * NEED, 128), 1) == who & 31
        value = jnp.sum(jnp.where(hit, found, 0.0), axis=1, keepdims=True)
        return jnp.broadcast_to(value, (N_WIN * NEED, 128))


    relay(1)
    pltpu.make_async_copy(far_masks, far_masks, m_recv.at[1]).wait()
    masks = mask_all[:, 0, :].astype(bf16)
    present[...] = availability_of(masks, work_row)
    final_present[...] = availability_of(masks, own_ref[pl.ds(me_p, 1), :])
    for s in range(2, STEPS):
        relay(s)
        if s >= 3:
            process(s - 3)
    for s in range(STEPS - 3, STEPS):
        process(s)

    lag_send[...] = acc[...].astype(bf16).reshape(N_WIN, SHARE, LAGS)

    def lagged(t):
        o = (me_w + t) % N_WIN
        return pltpu.make_async_remote_copy(
            src_ref=lag_send.at[o],
            dst_ref=lag_recv.at[z],
            send_sem=l_send.at[t],
            recv_sem=l_recv.at[z],
            device_id={"win": o, "pair": x * NZ + my_owner_z},
        )

    for t in (4, 3, 5, 2, 6, 1, 7):
        lagged(t).start()

    @pl.when(me_w == 1)
    def _():
        pltpu.make_async_copy(lag_send.at[me_w], lag_recv.at[z], l_recv.at[z]).start()

    @pl.when(me_w != 1)
    def _():
        lagged(0).start()

    counts = []
    for j in range(PC // N_WIN):
        count = jnp.zeros((PR, 128), f32)
        for w in range(N_WIN):
            column = pl.ds(NEED * w + PR + (PC // N_WIN) * me_w + j, 1)
            count = count + final_present[NEED * w : NEED * w + PR, :] * final_present[column, :]
        counts.append(count)
    count = jnp.maximum(jnp.concatenate(counts, axis=0)[:, :1], 1.0)

    total = jnp.zeros((SHARE, LAGS), f32)
    for k in range(NZ):
        piece = lag_recv.at[k]
        pltpu.make_async_copy(piece, piece, l_recv.at[k]).wait()
        total = total + lag_recv[k].astype(f32)
    out_ref[...] = total / count

    for s in range(STEPS):
        sent = recv1[s].at[pl.ds(0, NZ - 1)]
        pltpu.make_async_copy(sent, sent, d_send.at[s]).wait()
        sent = send2[s].at[pl.ds(0, PLANE - 1)]
        pltpu.make_async_copy(sent, sent, s_send.at[s]).wait()
    pltpu.make_async_copy(near_masks, near_masks, m_send.at[0]).wait()
    pltpu.make_async_copy(far_masks, far_masks, m_send.at[1]).wait()
    for t in range(1, N_WIN):
        lagged(t).wait_send()

    @pl.when(me_w != 1)
    def _():
        lagged(0).wait_send()


def per_device(spectra, availability, owners):
    dma = pltpu.SemaphoreType.DMA
    anywhere = pl.BlockSpec(memory_space=pl.ANY)
    out = pl.pallas_call(
        kernel,
        out_shape=jax.ShapeDtypeStruct((SHARE, LAGS), f32),
        in_specs=[anywhere] * 3,
        out_specs=pl.BlockSpec(memory_space=pltpu.VMEM),
        scratch_shapes=[
            pltpu.VMEM((BLOCK, 2, BINS), bf16),
            pltpu.VMEM((N_PAIR, NEED), i32),
            pltpu.VMEM((1, BLOCK), i32),
            pltpu.VMEM((N_WIN, 2, NEED, WIDEST), f32),
            pltpu.VMEM((2 * PAIRS, 2 * WIDEST), bf16),
            pltpu.VMEM((PAIRS, LAGS), f32),
            pltpu.VMEM((HALVES, 16 * N_PAIR, QUAD * 2 * BLOCK), bf16),
            pltpu.VMEM((CHUNK // FINE, LAGS), f32),
            pltpu.VMEM((CHUNK // FINE, LAGS), f32),
            pltpu.VMEM((NZ, 1, 128), f32),
            pltpu.VMEM((N_WIN * N_PAIR, 1, 128), f32),
            pltpu.VMEM((N_WIN * NEED, 128), f32),
            pltpu.VMEM((N_WIN * NEED, 128), f32),
            pltpu.VMEM((N_WIN, SHARE, LAGS), bf16),
            pltpu.VMEM((NZ, SHARE, LAGS), bf16),
            dma((3,)),
            dma((STEPS,)),
            dma((STEPS,)),
            dma((STEPS,)),
            dma((STEPS,)),
            dma((2,)),
            dma((2,)),
            dma((N_WIN,)),
            dma((NZ,)),
        ]
        + [pltpu.VMEM((NZ, BLOCK, 2, wide), bf16) for wide in WIDTHS]
        + [pltpu.VMEM((N_PAIR, MSG, wide), bf16) for wide in WIDTHS]
        + [pltpu.VMEM((PLANE, MSG, wide), bf16) for wide in WIDTHS]
        + [pltpu.VMEM((2 * wide, LAGS), bf16) for wide in WIDTHS],
        compiler_params=pltpu.CompilerParams(
            collective_id=0, has_side_effects=True, vmem_limit_bytes=48 * 1024 * 1024
        ),
        cost_estimate=pl.CostEstimate(
            flops=6_000_000_000, bytes_accessed=2_000_000, transcendentals=1_000_000
        ),
    )(spectra, owners, availability)
    return out.reshape(PC // N_WIN, PR, LAGS)


def solution(mesh):
    return jax.shard_map(
        per_device,
        mesh=mesh,
        in_specs=(P("win", "pair", None, None), P("win", "pair"), P()),
        out_specs=P("win", "pair", None),
        check_vma=False,
    )
```

```python
import math

import jax
import jax.numpy as jnp
from jax import lax
from jax.experimental import pallas as pl
from jax.experimental.pallas import tpu as pltpu
from jax.sharding import PartitionSpec as P

WB = 64
LAGS = 512
PR = 16
PC = 16
NEED = 32
EPSILON = 1e-06

NX, NZ = 4, 8
N_PAIR = NX * NZ
N_WIN = 8
BLOCK = 32
BINS = 8192
CHUNK = BINS // NZ
WIDTHS = (128,) * 8
STEPS = len(WIDTHS)
STARTS = tuple(sum(WIDTHS[:s]) for s in range(STEPS))
WIDEST = max(WIDTHS)
AHEAD = 4
PLANE = NX * N_WIN
HALVES = 2
QUAD = NZ // HALVES
MSG = 4 * NZ
PERIOD = 2 * BINS
FINE = 32
PAIRS = PC * PR
SHARE = PAIRS // N_WIN

f32 = jnp.float32
bf16 = jnp.bfloat16
i32 = jnp.int32

Z_OFFSETS = [4, 3, -3, 2, -2, 1, -1]
PLANE_OFFSETS = [(dw, dx) for dw in (4, 3, 5, 2, 6, 1, 7, 0) for dx in (2, 1, -1, 0)][:-1]


def iota(shape, dim):
    return lax.broadcasted_iota(i32, shape, dim)


def work_z(w, z):
    y, core = w // 2, w % 2
    near = jnp.where(y < 2, 4 - 2 * y, 3 - 2 * ((y + z) % 2))
    return (z + near + 4 * core) % NZ


def worker(offset, z):
    core = 0 if 1 <= offset <= 4 else 1
    near = offset - 4 * core
    near = near + NZ if near < 0 else near
    odd = z % 2
    y = {4: 0, 2: 1, 3: 2 + odd, 1: 3 - odd}[near]
    return 2 * y + core


def kernel(
    x_hbm,
    own_hbm,
    avail_hbm,
    out_ref,
    x_ref,
    own_ref,
    avail_ref,
    white,
    lhs,
    acc,
    smat,
    cos_a,
    sin_a,
    mask_z,
    mask_all,
    present,
    final_present,
    lag_send,
    lag_recv,
    in_sem,
    d_send,
    d_recv,
    s_send,
    s_recv,
    m_send,
    m_recv,
    l_send,
    l_recv,
    *steps,
):
    recv1, send2, recv2, table = (steps[STEPS * i : STEPS * (i + 1)] for i in range(4))
    me_w = lax.axis_index("win")
    me_p = lax.axis_index("pair")
    x, z = me_p // NZ, me_p % NZ
    z_peers = [(z + dz + NZ) % NZ for dz in Z_OFFSETS]
    my_owner_z = work_z(me_w, z)
    plane_peers = [((me_w + dw) % N_WIN, (x + dx + NX) % NX) for dw, dx in PLANE_OFFSETS]

    barrier = pltpu.get_barrier_semaphore()
    for k in z_peers:
        pl.semaphore_signal(barrier, inc=1, device_id={"pair": x * NZ + k})
    for o, k in plane_peers:
        pl.semaphore_signal(barrier, inc=1, device_id={"win": o, "pair": k * NZ + z})
    for offset in range(1, NZ):
        k = (z - offset + NZ) % NZ
        pl.semaphore_signal(
            barrier, inc=1, device_id={"win": worker(offset, k), "pair": x * NZ + k}
        )
    own_in = pltpu.make_async_copy(own_hbm, own_ref, in_sem.at[0])
    avail_in = pltpu.make_async_copy(avail_hbm, avail_ref, in_sem.at[1])
    x_in = pltpu.make_async_copy(x_hbm.at[0], x_ref, in_sem.at[2])
    own_in.start()
    avail_in.start()
    x_in.start()
    avail_in.wait()
    mask_z[z] = jnp.concatenate(
        [avail_ref[...].astype(f32), jnp.zeros((1, 128 - BLOCK), f32)], axis=1
    )
    x_in.wait()
    pl.semaphore_wait(barrier, NZ - 1 + PLANE - 1 + jnp.where(me_w == 1, 0, N_WIN))


    def spectra_step(s, k):
        bins = pl.ds(pl.multiple_of(k * CHUNK + STARTS[s], 128), WIDTHS[s])
        return x_ref.at[:, :, bins]

    def start_spectra(s):
        for k in z_peers:
            pltpu.make_async_remote_copy(
                src_ref=spectra_step(s, k),
                dst_ref=recv1[s].at[z],
                send_sem=d_send.at[s],
                recv_sem=d_recv.at[s],
                device_id={"pair": x * NZ + k},
            ).start()
        pltpu.make_async_copy(spectra_step(s, z), recv1[s].at[z], d_recv.at[s]).start()

    for k in z_peers:
        pltpu.make_async_remote_copy(
            src_ref=mask_z.at[z],
            dst_ref=mask_z.at[z],
            send_sem=m_send.at[0],
            recv_sem=m_recv.at[0],
            device_id={"pair": x * NZ + k},
        ).start()

    for s in range(AHEAD):
        start_spectra(s)
    own_in.wait()

    rows = 16 * N_PAIR
    owners = own_ref[...]
    spread = (iota((rows, N_PAIR), 0) >> 4 == iota((rows, N_PAIR), 1)).astype(bf16)
    block = jnp.dot(spread, (owners >> 5).astype(bf16), preferred_element_type=f32)
    station = jnp.dot(spread, (owners & 31).astype(bf16), preferred_element_type=f32)
    row = iota((rows, 1), 0)
    near = (row >> 2) & 3
    upper_slot = ((row >> 1) & 1) == 1
    for half in range(HALVES):
        mine = block == (x * NZ + half * QUAD + near).astype(f32)
        first = jnp.min(jnp.where(mine, station, BLOCK - 1.0), axis=1, keepdims=True)
        last = jnp.max(jnp.where(mine, station, 0.0), axis=1, keepdims=True)
        wanted = jnp.where(upper_slot, last, first).astype(i32)
        source = near * (2 * BLOCK) + 2 * wanted + (row & 1)
        smat[half] = (iota((rows, QUAD * 2 * BLOCK), 1) == source).astype(bf16)

    near_masks = mask_z.at[pl.ds(0, NZ - 1)]
    pltpu.make_async_copy(near_masks, near_masks, m_recv.at[0]).wait()
    here = pl.ds((me_w * NX + x) * NZ, NZ)
    for o, k in plane_peers:
        pltpu.make_async_remote_copy(
            src_ref=mask_z,
            dst_ref=mask_all.at[here],
            send_sem=m_send.at[1],
            recv_sem=m_recv.at[1],
            device_id={"win": o, "pair": k * NZ + z},
        ).start()
    mask_all[here] = mask_z[...]
    far_masks = mask_all.at[pl.ds(0, N_WIN * N_PAIR - NZ)]

    def relay(s):
        whole = recv1[s]
        pltpu.make_async_copy(whole, whole, d_recv.at[s]).wait()

        if s + AHEAD < STEPS:
            start_spectra(s + AHEAD)

        for half in range(HALVES):
            stations = recv1[s][half * QUAD : (half + 1) * QUAD]
            stations = stations.reshape(QUAD * 2 * BLOCK, WIDTHS[s])
            message = jnp.dot(smat[half], stations, preferred_element_type=f32).astype(bf16)
            send2[s][:, 16 * half : 16 * (half + 1), :] = message.reshape(N_PAIR, 16, WIDTHS[s])
        for o, k in plane_peers:
            pltpu.make_async_remote_copy(
                src_ref=send2[s].at[k * NZ + work_z(o, z)],
                dst_ref=recv2[s].at[me_w * NX + x],
                send_sem=s_send.at[s],
                recv_sem=s_recv.at[s],
                device_id={"win": o, "pair": k * NZ + z},
            ).start()
        recv2[s][me_w * NX + x] = send2[s][x * NZ + my_owner_z]

    def process(s):
        wide = WIDTHS[s]
        others = recv2[s].at[pl.ds(0, PLANE - 1)]
        pltpu.make_async_copy(others, others, s_recv.at[s]).wait()
        res, ims, magnitudes = [], [], []
        for w in range(N_WIN):
            messages = recv2[s][NX * w : NX * (w + 1)].reshape(NX * MSG, wide)
            lines = jnp.dot(rmat, messages, preferred_element_type=f32)
            res.append(lines[:NEED])
            ims.append(lines[NEED:])
            magnitudes.append(jnp.sqrt(res[w] * res[w] + ims[w] * ims[w]))
        magnitude = jnp.concatenate(magnitudes, axis=0)
        upper = magnitude.astype(bf16)
        lower = (magnitude - upper.astype(f32)).astype(bf16)
        both = jnp.concatenate([upper, lower], axis=0)
        levels = jnp.dot(both, band[:wide, :wide], preferred_element_type=f32)
        level = levels[: N_WIN * NEED] + levels[N_WIN * NEED :]
        factor = present[:, :1] / (level + EPSILON)
        for w in range(N_WIN):
            own = factor[NEED * w : NEED * (w + 1)]
            white[w, 0, :, :wide] = (res[w] * own).astype(bf16).astype(f32)
            white[w, 1, :, :wide] = (ims[w] * own).astype(bf16).astype(f32)
        for j in range(PC):
            total_re = jnp.zeros((PR, wide), f32)
            total_im = jnp.zeros((PR, wide), f32)
            for w in range(N_WIN):
                ar, ai = white[w, 0, :PR, :wide], white[w, 1, :PR, :wide]
                br = white[w, 0, PR + j : PR + j + 1, :wide]
                bi = white[w, 1, PR + j : PR + j + 1, :wide]
                total_re = total_re + (ar * br + ai * bi)
                total_im = total_im + (ai * br - ar * bi)
            for part, total in enumerate((total_re, total_im)):
                upper = total.astype(bf16)
                lower = (total - upper.astype(f32)).astype(bf16)
                lhs[PR * j : PR * (j + 1), wide * part : wide * (part + 1)] = upper
                lhs[PAIRS + PR * j : PAIRS + PR * (j + 1), wide * part : wide * (part + 1)] = lower
        product = jnp.dot(lhs[:, : 2 * wide], table[s][...], preferred_element_type=f32)
        acc[...] += product[:PAIRS] + product[PAIRS:]

    relay(0)

    lag = iota((FINE, LAGS), 1) - LAGS // 2
    index = iota((FINE, LAGS), 0)

    def angle(phase):
        phase = ((phase + PERIOD // 2) & (PERIOD - 1)) - PERIOD // 2
        return phase.astype(f32) * (2.0 * math.pi / PERIOD)

    coarse = angle((z * CHUNK + FINE * index) * lag)
    cos_a[...] = jnp.cos(coarse)
    sin_a[...] = jnp.sin(coarse)
    fine = angle(index * lag)
    cos_b, sin_b = jnp.cos(fine), jnp.sin(fine)

    for s in range(STEPS):

        def table_rows(n, carry, s=s):
            at = STARTS[s] // FINE + n
            ca, sa = cos_a[pl.ds(at, 1), :], sin_a[pl.ds(at, 1), :]
            bins = z * CHUNK + FINE * at + iota((FINE, 1), 0)
            weight = jnp.where(bins == 0, 1.0, 2.0) / math.sqrt(PERIOD)
            real = pl.ds(pl.multiple_of(n * FINE, FINE), FINE)
            imag = pl.ds(pl.multiple_of(WIDTHS[s] + n * FINE, FINE), FINE)
            table[s][real, :] = (weight * (ca * cos_b - sa * sin_b)).astype(bf16)
            table[s][imag, :] = (-weight * (sa * cos_b + ca * sin_b)).astype(bf16)
            return carry

        lax.fori_loop(0, WIDTHS[s] // FINE, table_rows, 0)

    def pick(count, lane, own_row):
        hit = iota((count, NEED), 1) == lane
        return jnp.sum(jnp.where(hit, own_row, 0), axis=1, keepdims=True)

    work_row = own_ref[pl.ds(x * NZ + my_owner_z, 1), :]
    sel = iota((2 * NEED, 1), 0)
    chosen = pick(2 * NEED, sel & (NEED - 1), work_row)
    earlier = jnp.logical_and(work_row >> 5 == chosen >> 5, work_row < chosen)
    slot = jnp.max(earlier.astype(f32), axis=1, keepdims=True).astype(i32)
    target = (chosen >> 5) * 4 + slot * 2 + (sel >> 5)
    rmat = (iota((2 * NEED, NX * MSG), 1) == target).astype(bf16)
    band = jnp.where(iota((WIDEST, WIDEST), 0) >> 6 == iota((WIDEST, WIDEST), 1) >> 6, 1.0 / WB, 0.0)
    band = band.astype(bf16)
    acc[...] = jnp.zeros_like(acc)

    line = iota((N_WIN * NEED, 1), 0)

    def availability_of(masks, own_row):
        who = pick(N_WIN * NEED, line & (NEED - 1), own_row)
        place = (line >> 5) * N_PAIR + (who >> 5)
        where = (iota((N_WIN * NEED, N_WIN * N_PAIR), 1) == place).astype(bf16)
        found = jnp.dot(where, masks, preferred_element_type=f32)
        hit = iota((N_WIN * NEED, 128), 1) == who & 31
        value = jnp.sum(jnp.where(hit, found, 0.0), axis=1, keepdims=True)
        return jnp.broadcast_to(value, (N_WIN * NEED, 128))


    relay(1)
    pltpu.make_async_copy(far_masks, far_masks, m_recv.at[1]).wait()
    masks = mask_all[:, 0, :].astype(bf16)
    present[...] = availability_of(masks, work_row)
    final_present[...] = availability_of(masks, own_ref[pl.ds(me_p, 1), :])
    for s in range(2, STEPS):
        relay(s)
        if s >= 4:
            process(s - 4)
    for s in range(STEPS - 4, STEPS):
        process(s)

    lag_send[...] = acc[...].astype(bf16).reshape(N_WIN, SHARE, LAGS)

    def lagged(t):
        o = (me_w + t) % N_WIN
        return pltpu.make_async_remote_copy(
            src_ref=lag_send.at[o],
            dst_ref=lag_recv.at[z],
            send_sem=l_send.at[t],
            recv_sem=l_recv.at[z],
            device_id={"win": o, "pair": x * NZ + my_owner_z},
        )

    for t in (4, 3, 5, 2, 6, 1, 7):
        lagged(t).start()

    @pl.when(me_w == 1)
    def _():
        pltpu.make_async_copy(lag_send.at[me_w], lag_recv.at[z], l_recv.at[z]).start()

    @pl.when(me_w != 1)
    def _():
        lagged(0).start()

    counts = []
    for j in range(PC // N_WIN):
        count = jnp.zeros((PR, 128), f32)
        for w in range(N_WIN):
            column = pl.ds(NEED * w + PR + (PC // N_WIN) * me_w + j, 1)
            count = count + final_present[NEED * w : NEED * w + PR, :] * final_present[column, :]
        counts.append(count)
    count = jnp.maximum(jnp.concatenate(counts, axis=0)[:, :1], 1.0)

    total = jnp.zeros((SHARE, LAGS), f32)
    for k in range(NZ):
        piece = lag_recv.at[k]
        pltpu.make_async_copy(piece, piece, l_recv.at[k]).wait()
        total = total + lag_recv[k].astype(f32)
    out_ref[...] = total / count

    for s in range(STEPS):
        sent = recv1[s].at[pl.ds(0, NZ - 1)]
        pltpu.make_async_copy(sent, sent, d_send.at[s]).wait()
        sent = send2[s].at[pl.ds(0, PLANE - 1)]
        pltpu.make_async_copy(sent, sent, s_send.at[s]).wait()
    pltpu.make_async_copy(near_masks, near_masks, m_send.at[0]).wait()
    pltpu.make_async_copy(far_masks, far_masks, m_send.at[1]).wait()
    for t in range(1, N_WIN):
        lagged(t).wait_send()

    @pl.when(me_w != 1)
    def _():
        lagged(0).wait_send()


def per_device(spectra, availability, owners):
    dma = pltpu.SemaphoreType.DMA
    anywhere = pl.BlockSpec(memory_space=pl.ANY)
    out = pl.pallas_call(
        kernel,
        out_shape=jax.ShapeDtypeStruct((SHARE, LAGS), f32),
        in_specs=[anywhere] * 3,
        out_specs=pl.BlockSpec(memory_space=pltpu.VMEM),
        scratch_shapes=[
            pltpu.VMEM((BLOCK, 2, BINS), bf16),
            pltpu.VMEM((N_PAIR, NEED), i32),
            pltpu.VMEM((1, BLOCK), i32),
            pltpu.VMEM((N_WIN, 2, NEED, WIDEST), f32),
            pltpu.VMEM((2 * PAIRS, 2 * WIDEST), bf16),
            pltpu.VMEM((PAIRS, LAGS), f32),
            pltpu.VMEM((HALVES, 16 * N_PAIR, QUAD * 2 * BLOCK), bf16),
            pltpu.VMEM((CHUNK // FINE, LAGS), f32),
            pltpu.VMEM((CHUNK // FINE, LAGS), f32),
            pltpu.VMEM((NZ, 1, 128), f32),
            pltpu.VMEM((N_WIN * N_PAIR, 1, 128), f32),
            pltpu.VMEM((N_WIN * NEED, 128), f32),
            pltpu.VMEM((N_WIN * NEED, 128), f32),
            pltpu.VMEM((N_WIN, SHARE, LAGS), bf16),
            pltpu.VMEM((NZ, SHARE, LAGS), bf16),
            dma((3,)),
            dma((STEPS,)),
            dma((STEPS,)),
            dma((STEPS,)),
            dma((STEPS,)),
            dma((2,)),
            dma((2,)),
            dma((N_WIN,)),
            dma((NZ,)),
        ]
        + [pltpu.VMEM((NZ, BLOCK, 2, wide), bf16) for wide in WIDTHS]
        + [pltpu.VMEM((N_PAIR, MSG, wide), bf16) for wide in WIDTHS]
        + [pltpu.VMEM((PLANE, MSG, wide), bf16) for wide in WIDTHS]
        + [pltpu.VMEM((2 * wide, LAGS), bf16) for wide in WIDTHS],
        compiler_params=pltpu.CompilerParams(
            collective_id=0, has_side_effects=True, vmem_limit_bytes=48 * 1024 * 1024
        ),
        cost_estimate=pl.CostEstimate(
            flops=6_000_000_000, bytes_accessed=2_000_000, transcendentals=1_000_000
        ),
    )(spectra, owners, availability)
    return out.reshape(PC // N_WIN, PR, LAGS)


def solution(mesh):
    return jax.shard_map(
        per_device,
        mesh=mesh,
        in_specs=(P("win", "pair", None, None), P("win", "pair"), P()),
        out_specs=P("win", "pair", None),
        check_vma=False,
    )
```

```python
import math

import jax
import jax.numpy as jnp
from jax import lax
from jax.experimental import pallas as pl
from jax.experimental.pallas import tpu as pltpu
from jax.sharding import PartitionSpec as P

WB = 64
LAGS = 512
PR = 16
PC = 16
NEED = 32
EPSILON = 1e-06

NX, NZ = 4, 8
N_PAIR = NX * NZ
N_WIN = 8
BLOCK = 32
BINS = 8192
CHUNK = BINS // NZ
WIDTHS = (128,) * 8
STEPS = len(WIDTHS)
STARTS = tuple(sum(WIDTHS[:s]) for s in range(STEPS))
WIDEST = max(WIDTHS)
AHEAD = 4
PLANE = NX * N_WIN
HALVES = 2
QUAD = NZ // HALVES
MSG = 4 * NZ
PERIOD = 2 * BINS
FINE = 32
PAIRS = PC * PR
SHARE = PAIRS // N_WIN

f32 = jnp.float32
bf16 = jnp.bfloat16
i32 = jnp.int32

Z_OFFSETS = [4, 3, -3, 2, -2, 1, -1]
PLANE_OFFSETS = [(dw, dx) for dw in (4, 3, 5, 2, 6, 1, 7, 0) for dx in (2, 1, -1, 0)][:-1]


def iota(shape, dim):
    return lax.broadcasted_iota(i32, shape, dim)


def work_z(w, z):
    y, core = w // 2, w % 2
    near = jnp.where(y < 2, 4 - 2 * y, 3 - 2 * ((y + z) % 2))
    return (z + near + 4 * core) % NZ


def worker(offset, z):
    core = 0 if 1 <= offset <= 4 else 1
    near = offset - 4 * core
    near = near + NZ if near < 0 else near
    odd = z % 2
    y = {4: 0, 2: 1, 3: 2 + odd, 1: 3 - odd}[near]
    return 2 * y + core


def kernel(
    x_hbm,
    own_hbm,
    avail_hbm,
    out_ref,
    x_ref,
    own_ref,
    avail_ref,
    white,
    lhs,
    acc,
    smat,
    cos_a,
    sin_a,
    mask_z,
    mask_all,
    present,
    final_present,
    lag_send,
    lag_recv,
    in_sem,
    d_send,
    d_recv,
    s_send,
    s_recv,
    m_send,
    m_recv,
    l_send,
    l_recv,
    *steps,
):
    recv1, send2, recv2, table = (steps[STEPS * i : STEPS * (i + 1)] for i in range(4))
    me_w = lax.axis_index("win")
    me_p = lax.axis_index("pair")
    x, z = me_p // NZ, me_p % NZ
    z_peers = [(z + dz + NZ) % NZ for dz in Z_OFFSETS]
    my_owner_z = work_z(me_w, z)
    plane_peers = [((me_w + dw) % N_WIN, (x + dx + NX) % NX) for dw, dx in PLANE_OFFSETS]

    barrier = pltpu.get_barrier_semaphore()
    for k in z_peers:
        pl.semaphore_signal(barrier, inc=1, device_id={"pair": x * NZ + k})
    for o, k in plane_peers:
        pl.semaphore_signal(barrier, inc=1, device_id={"win": o, "pair": k * NZ + z})
    for offset in range(1, NZ):
        k = (z - offset + NZ) % NZ
        pl.semaphore_signal(
            barrier, inc=1, device_id={"win": worker(offset, k), "pair": x * NZ + k}
        )
    own_in = pltpu.make_async_copy(own_hbm, own_ref, in_sem.at[0])
    avail_in = pltpu.make_async_copy(avail_hbm, avail_ref, in_sem.at[1])
    x_in = pltpu.make_async_copy(x_hbm.at[0], x_ref, in_sem.at[2])
    own_in.start()
    avail_in.start()
    x_in.start()
    avail_in.wait()
    mask_z[z] = jnp.concatenate(
        [avail_ref[...].astype(f32), jnp.zeros((1, 128 - BLOCK), f32)], axis=1
    )
    x_in.wait()
    pl.semaphore_wait(barrier, NZ - 1 + PLANE - 1 + jnp.where(me_w == 1, 0, N_WIN))


    def spectra_step(s, k):
        bins = pl.ds(pl.multiple_of(k * CHUNK + STARTS[s], 128), WIDTHS[s])
        return x_ref.at[:, :, bins]

    def start_spectra(s):
        for k in z_peers:
            pltpu.make_async_remote_copy(
                src_ref=spectra_step(s, k),
                dst_ref=recv1[s].at[z],
                send_sem=d_send.at[s],
                recv_sem=d_recv.at[s],
                device_id={"pair": x * NZ + k},
            ).start()
        pltpu.make_async_copy(spectra_step(s, z), recv1[s].at[z], d_recv.at[s]).start()

    for k in z_peers:
        pltpu.make_async_remote_copy(
            src_ref=mask_z.at[z],
            dst_ref=mask_z.at[z],
            send_sem=m_send.at[0],
            recv_sem=m_recv.at[0],
            device_id={"pair": x * NZ + k},
        ).start()

    for s in range(AHEAD):
        start_spectra(s)
    own_in.wait()

    rows = 16 * N_PAIR
    owners = own_ref[...]
    spread = (iota((rows, N_PAIR), 0) >> 4 == iota((rows, N_PAIR), 1)).astype(bf16)
    block = jnp.dot(spread, (owners >> 5).astype(bf16), preferred_element_type=f32)
    station = jnp.dot(spread, (owners & 31).astype(bf16), preferred_element_type=f32)
    row = iota((rows, 1), 0)
    near = (row >> 2) & 3
    upper_slot = ((row >> 1) & 1) == 1
    for half in range(HALVES):
        mine = block == (x * NZ + half * QUAD + near).astype(f32)
        first = jnp.min(jnp.where(mine, station, BLOCK - 1.0), axis=1, keepdims=True)
        last = jnp.max(jnp.where(mine, station, 0.0), axis=1, keepdims=True)
        wanted = jnp.where(upper_slot, last, first).astype(i32)
        source = near * (2 * BLOCK) + 2 * wanted + (row & 1)
        smat[half] = (iota((rows, QUAD * 2 * BLOCK), 1) == source).astype(bf16)

    near_masks = mask_z.at[pl.ds(0, NZ - 1)]
    pltpu.make_async_copy(near_masks, near_masks, m_recv.at[0]).wait()
    here = pl.ds((me_w * NX + x) * NZ, NZ)
    for o, k in plane_peers:
        pltpu.make_async_remote_copy(
            src_ref=mask_z,
            dst_ref=mask_all.at[here],
            send_sem=m_send.at[1],
            recv_sem=m_recv.at[1],
            device_id={"win": o, "pair": k * NZ + z},
        ).start()
    mask_all[here] = mask_z[...]
    far_masks = mask_all.at[pl.ds(0, N_WIN * N_PAIR - NZ)]

    def relay(s):
        whole = recv1[s]
        pltpu.make_async_copy(whole, whole, d_recv.at[s]).wait()

        if s + AHEAD < STEPS:
            start_spectra(s + AHEAD)

        for half in range(HALVES):
            stations = recv1[s][half * QUAD : (half + 1) * QUAD]
            stations = stations.reshape(QUAD * 2 * BLOCK, WIDTHS[s])
            message = jnp.dot(smat[half], stations, preferred_element_type=f32).astype(bf16)
            send2[s][:, 16 * half : 16 * (half + 1), :] = message.reshape(N_PAIR, 16, WIDTHS[s])
        for o, k in plane_peers:
            pltpu.make_async_remote_copy(
                src_ref=send2[s].at[k * NZ + work_z(o, z)],
                dst_ref=recv2[s].at[me_w * NX + x],
                send_sem=s_send.at[s],
                recv_sem=s_recv.at[s],
                device_id={"win": o, "pair": k * NZ + z},
            ).start()
        recv2[s][me_w * NX + x] = send2[s][x * NZ + my_owner_z]

    def process(s):
        wide = WIDTHS[s]
        others = recv2[s].at[pl.ds(0, PLANE - 1)]
        pltpu.make_async_copy(others, others, s_recv.at[s]).wait()
        res, ims, magnitudes = [], [], []
        for w in range(N_WIN):
            messages = recv2[s][NX * w : NX * (w + 1)].reshape(NX * MSG, wide)
            lines = jnp.dot(rmat, messages, preferred_element_type=f32)
            res.append(lines[:NEED])
            ims.append(lines[NEED:])
            magnitudes.append(jnp.sqrt(res[w] * res[w] + ims[w] * ims[w]))
        magnitude = jnp.concatenate(magnitudes, axis=0)
        upper = magnitude.astype(bf16)
        lower = (magnitude - upper.astype(f32)).astype(bf16)
        both = jnp.concatenate([upper, lower], axis=0)
        levels = jnp.dot(both, band[:wide, :wide], preferred_element_type=f32)
        level = levels[: N_WIN * NEED] + levels[N_WIN * NEED :]
        factor = present[:, :1] / (level + EPSILON)
        for w in range(N_WIN):
            own = factor[NEED * w : NEED * (w + 1)]
            white[w, 0, :, :wide] = (res[w] * own).astype(bf16).astype(f32)
            white[w, 1, :, :wide] = (ims[w] * own).astype(bf16).astype(f32)
        for j in range(PC):
            total_re = jnp.zeros((PR, wide), f32)
            total_im = jnp.zeros((PR, wide), f32)
            for w in range(N_WIN):
                ar, ai = white[w, 0, :PR, :wide], white[w, 1, :PR, :wide]
                br = white[w, 0, PR + j : PR + j + 1, :wide]
                bi = white[w, 1, PR + j : PR + j + 1, :wide]
                total_re = total_re + (ar * br + ai * bi)
                total_im = total_im + (ai * br - ar * bi)
            for part, total in enumerate((total_re, total_im)):
                upper = total.astype(bf16)
                lower = (total - upper.astype(f32)).astype(bf16)
                lhs[PR * j : PR * (j + 1), wide * part : wide * (part + 1)] = upper
                lhs[PAIRS + PR * j : PAIRS + PR * (j + 1), wide * part : wide * (part + 1)] = lower
        product = jnp.dot(lhs[:, : 2 * wide], table[s][...], preferred_element_type=f32)
        acc[...] += product[:PAIRS] + product[PAIRS:]

    relay(0)

    lag = iota((FINE, LAGS), 1) - LAGS // 2
    index = iota((FINE, LAGS), 0)

    def angle(phase):
        phase = ((phase + PERIOD // 2) & (PERIOD - 1)) - PERIOD // 2
        return phase.astype(f32) * (2.0 * math.pi / PERIOD)

    coarse = angle((z * CHUNK + FINE * index) * lag)
    cos_a[...] = jnp.cos(coarse)
    sin_a[...] = jnp.sin(coarse)
    fine = angle(index * lag)
    cos_b, sin_b = jnp.cos(fine), jnp.sin(fine)

    for s in range(STEPS):

        def table_rows(n, carry, s=s):
            at = STARTS[s] // FINE + n
            ca, sa = cos_a[pl.ds(at, 1), :], sin_a[pl.ds(at, 1), :]
            bins = z * CHUNK + FINE * at + iota((FINE, 1), 0)
            weight = jnp.where(bins == 0, 1.0, 2.0) / math.sqrt(PERIOD)
            real = pl.ds(pl.multiple_of(n * FINE, FINE), FINE)
            imag = pl.ds(pl.multiple_of(WIDTHS[s] + n * FINE, FINE), FINE)
            table[s][real, :] = (weight * (ca * cos_b - sa * sin_b)).astype(bf16)
            table[s][imag, :] = (-weight * (sa * cos_b + ca * sin_b)).astype(bf16)
            return carry

        lax.fori_loop(0, WIDTHS[s] // FINE, table_rows, 0)

    def pick(count, lane, own_row):
        hit = iota((count, NEED), 1) == lane
        return jnp.sum(jnp.where(hit, own_row, 0), axis=1, keepdims=True)

    work_row = own_ref[pl.ds(x * NZ + my_owner_z, 1), :]
    sel = iota((2 * NEED, 1), 0)
    chosen = pick(2 * NEED, sel & (NEED - 1), work_row)
    earlier = jnp.logical_and(work_row >> 5 == chosen >> 5, work_row < chosen)
    slot = jnp.max(earlier.astype(f32), axis=1, keepdims=True).astype(i32)
    target = (chosen >> 5) * 4 + slot * 2 + (sel >> 5)
    rmat = (iota((2 * NEED, NX * MSG), 1) == target).astype(bf16)
    band = jnp.where(iota((WIDEST, WIDEST), 0) >> 6 == iota((WIDEST, WIDEST), 1) >> 6, 1.0 / WB, 0.0)
    band = band.astype(bf16)
    acc[...] = jnp.zeros_like(acc)

    line = iota((N_WIN * NEED, 1), 0)

    def availability_of(masks, own_row):
        who = pick(N_WIN * NEED, line & (NEED - 1), own_row)
        place = (line >> 5) * N_PAIR + (who >> 5)
        where = (iota((N_WIN * NEED, N_WIN * N_PAIR), 1) == place).astype(bf16)
        found = jnp.dot(where, masks, preferred_element_type=f32)
        hit = iota((N_WIN * NEED, 128), 1) == who & 31
        value = jnp.sum(jnp.where(hit, found, 0.0), axis=1, keepdims=True)
        return jnp.broadcast_to(value, (N_WIN * NEED, 128))


    relay(1)
    pltpu.make_async_copy(far_masks, far_masks, m_recv.at[1]).wait()
    masks = mask_all[:, 0, :].astype(bf16)
    present[...] = availability_of(masks, work_row)
    final_present[...] = availability_of(masks, own_ref[pl.ds(me_p, 1), :])
    for s in range(2, STEPS):
        relay(s)
        if s >= 4:
            process(s - 4)
    for s in range(STEPS - 4, STEPS):
        process(s)

    lag_send[...] = acc[...].astype(bf16).reshape(N_WIN, SHARE, LAGS)

    def lagged(t):
        o = (me_w + t) % N_WIN
        return pltpu.make_async_remote_copy(
            src_ref=lag_send.at[o],
            dst_ref=lag_recv.at[z],
            send_sem=l_send.at[t],
            recv_sem=l_recv.at[z],
            device_id={"win": o, "pair": x * NZ + my_owner_z},
        )

    for t in (1, 7, 2, 6, 3, 5, 4):
        lagged(t).start()

    @pl.when(me_w == 1)
    def _():
        pltpu.make_async_copy(lag_send.at[me_w], lag_recv.at[z], l_recv.at[z]).start()

    @pl.when(me_w != 1)
    def _():
        lagged(0).start()

    counts = []
    for j in range(PC // N_WIN):
        count = jnp.zeros((PR, 128), f32)
        for w in range(N_WIN):
            column = pl.ds(NEED * w + PR + (PC // N_WIN) * me_w + j, 1)
            count = count + final_present[NEED * w : NEED * w + PR, :] * final_present[column, :]
        counts.append(count)
    count = jnp.maximum(jnp.concatenate(counts, axis=0)[:, :1], 1.0)

    total = jnp.zeros((SHARE, LAGS), f32)
    for k in range(NZ):
        piece = lag_recv.at[k]
        pltpu.make_async_copy(piece, piece, l_recv.at[k]).wait()
        total = total + lag_recv[k].astype(f32)
    out_ref[...] = total / count

    for s in range(STEPS):
        sent = recv1[s].at[pl.ds(0, NZ - 1)]
        pltpu.make_async_copy(sent, sent, d_send.at[s]).wait()
        sent = send2[s].at[pl.ds(0, PLANE - 1)]
        pltpu.make_async_copy(sent, sent, s_send.at[s]).wait()
    pltpu.make_async_copy(near_masks, near_masks, m_send.at[0]).wait()
    pltpu.make_async_copy(far_masks, far_masks, m_send.at[1]).wait()
    for t in range(1, N_WIN):
        lagged(t).wait_send()

    @pl.when(me_w != 1)
    def _():
        lagged(0).wait_send()


def per_device(spectra, availability, owners):
    dma = pltpu.SemaphoreType.DMA
    anywhere = pl.BlockSpec(memory_space=pl.ANY)
    out = pl.pallas_call(
        kernel,
        out_shape=jax.ShapeDtypeStruct((SHARE, LAGS), f32),
        in_specs=[anywhere] * 3,
        out_specs=pl.BlockSpec(memory_space=pltpu.VMEM),
        scratch_shapes=[
            pltpu.VMEM((BLOCK, 2, BINS), bf16),
            pltpu.VMEM((N_PAIR, NEED), i32),
            pltpu.VMEM((1, BLOCK), i32),
            pltpu.VMEM((N_WIN, 2, NEED, WIDEST), f32),
            pltpu.VMEM((2 * PAIRS, 2 * WIDEST), bf16),
            pltpu.VMEM((PAIRS, LAGS), f32),
            pltpu.VMEM((HALVES, 16 * N_PAIR, QUAD * 2 * BLOCK), bf16),
            pltpu.VMEM((CHUNK // FINE, LAGS), f32),
            pltpu.VMEM((CHUNK // FINE, LAGS), f32),
            pltpu.VMEM((NZ, 1, 128), f32),
            pltpu.VMEM((N_WIN * N_PAIR, 1, 128), f32),
            pltpu.VMEM((N_WIN * NEED, 128), f32),
            pltpu.VMEM((N_WIN * NEED, 128), f32),
            pltpu.VMEM((N_WIN, SHARE, LAGS), bf16),
            pltpu.VMEM((NZ, SHARE, LAGS), bf16),
            dma((3,)),
            dma((STEPS,)),
            dma((STEPS,)),
            dma((STEPS,)),
            dma((STEPS,)),
            dma((2,)),
            dma((2,)),
            dma((N_WIN,)),
            dma((NZ,)),
        ]
        + [pltpu.VMEM((NZ, BLOCK, 2, wide), bf16) for wide in WIDTHS]
        + [pltpu.VMEM((N_PAIR, MSG, wide), bf16) for wide in WIDTHS]
        + [pltpu.VMEM((PLANE, MSG, wide), bf16) for wide in WIDTHS]
        + [pltpu.VMEM((2 * wide, LAGS), bf16) for wide in WIDTHS],
        compiler_params=pltpu.CompilerParams(
            collective_id=0, has_side_effects=True, vmem_limit_bytes=48 * 1024 * 1024
        ),
        cost_estimate=pl.CostEstimate(
            flops=6_000_000_000, bytes_accessed=2_000_000, transcendentals=1_000_000
        ),
    )(spectra, owners, availability)
    return out.reshape(PC // N_WIN, PR, LAGS)


def solution(mesh):
    return jax.shard_map(
        per_device,
        mesh=mesh,
        in_specs=(P("win", "pair", None, None), P("win", "pair"), P()),
        out_specs=P("win", "pair", None),
        check_vma=False,
    )
```
